32 devices in a mesh: parts: 2 (over y), blk: 4 (over z), rows: 4 (over x, core).
Axes of the slice: x: 2, y: 2, z: 4, core: 2. Of those that a mesh axis runs over, the one named last changes fastest.
Arguments:
- tiles: float32 [16, 1024, 1024], P(('parts', 'blk'), 'rows'), parts along dimension 0, may hold values from -6 to 6
- pairs: int32 [8, 2, 2], P(('parts', 'blk')), parts along dimension 0, may hold values from 0 to 3, as said below
- counts: int32 [8], P(('parts', 'blk')), parts along dimension 0, may hold values from 1 to 2, as said below
Outputs:
- surfaces: float32 [16, 1024, 1024], P(('parts', 'blk'), 'rows'), parts along dimension 0
The draws below stay inside these ranges and needn't reach their ends.
There are 2 independent parts, one for each index of `parts`. The reference program is written for one: setup_inputs(seed, part) draws one part's arguments, and reference() takes and returns one part's arrays. A program takes and returns all parts, laid end to end along the dimension named above; each array names one. Nothing has to cross between parts.
Inputs may be any that keep to these rules, and one draw needn't show every extreme that they name: pairs[b, k] = (a, c) with a < 2; c below 2 names a tile of group b, otherwise a tile of the group half the groups away; slot 0 of every group names a tile of that other group. Slots k < counts[b] of group b are live; some group has all 2 slots live.
All inputs are finite; a program needn't handle non-finite values.
Results may differ from the reference program's by a relative error of at most 0.011.
Values may be sent and summed in bfloat16 or wider, within the bound.
A program may use at most 64 MiB of HBM per device.

```python
import math
import jax
import jax.numpy as jnp
from jax import lax

H = 1024
W = 1024
TILES_DEV = 2
PAIR_CAP = 2
TILES = 8
N_BLK = 4


def draw_pairs(key, part):
    first_key = jax.random.fold_in(key, 11)
    second_key = jax.random.fold_in(key, 12)
    first = jax.random.randint(first_key, (N_BLK, PAIR_CAP), 0, TILES_DEV)
    second = jax.random.randint(second_key, (N_BLK, PAIR_CAP), 0, 2 * TILES_DEV)
    slot = jnp.arange(PAIR_CAP, dtype=jnp.int32)[None, :]
    second = jnp.where(slot == 0, TILES_DEV + second % TILES_DEV, second)
    return jnp.stack([first, second], axis=2).astype(jnp.int32)


def draw_counts(key, part):
    count_key = jax.random.fold_in(key, 21)
    pick_key = jax.random.fold_in(key, 22)
    drawn = jax.random.randint(count_key, (N_BLK,), 1, PAIR_CAP + 1)
    chosen = jax.random.randint(pick_key, (), 0, N_BLK)
    group = jnp.arange(N_BLK, dtype=jnp.int32)
    return jnp.where(group == chosen, PAIR_CAP, drawn).astype(jnp.int32)


def steps_of(key, shape, cuts, least, largest):
    level = 1.0
    for axis_at, shards_of in cuts:
        draws = jax.random.uniform(jax.random.fold_in(jax.random.fold_in(key, 6), axis_at), (shards_of,), jnp.float32, least / len(cuts), largest / len(cuts))
        level = level * jnp.repeat(jnp.exp(draws), shape[axis_at] // shards_of).reshape((-1,) + (1,) * (len(shape) - 1 - axis_at))
    return level


def bell_draw(rng, dims, scale, reach, cuts=(), kind=jnp.bfloat16):
    level = steps_of(rng, dims, cuts, -0.22, 0.18) if cuts else 1.0
    values = jax.random.normal(rng, dims, jnp.float32) * scale * level
    return jnp.minimum(jnp.maximum(values, -reach), reach).astype(kind)


def setup_inputs(seed: int = 0, part: int = 0) -> dict:
    splits = jax.random.split(jax.random.key(seed), 4)
    part_keys = jax.random.split(jax.random.fold_in(splits[3], part), 4)
    tiles = bell_draw(part_keys[0], (TILES, H, W), 1.0, 6.0, ((0, 4), (1, 4)), jnp.float32)
    pairs = draw_pairs(jax.random.fold_in(jax.random.fold_in(splits[3], part), 71), part)
    counts = draw_counts(jax.random.fold_in(jax.random.fold_in(splits[3], part), 71), part)
    return {"tiles": tiles, "pairs": pairs, "counts": counts}


FLOOR = 0.05

def dft_tables(length):
    index = jnp.arange(length, dtype=jnp.int32)
    phase = index[:, None] * index[None, :] % length
    angle = 2.0 * math.pi / length * phase.astype(jnp.float32)
    factor = 1.0 / math.sqrt(length)
    return ((jnp.cos(angle) * factor).astype(jnp.bfloat16), (jnp.sin(angle) * factor).astype(jnp.bfloat16))

def hann(length, first, number):
    index = (first + jnp.arange(number, dtype=jnp.int32)).astype(jnp.float32)
    return 0.5 - 0.5 * jnp.cos(2.0 * math.pi / length * index)

def reference(tiles, pairs, counts):
    cos_h, sin_h = dft_tables(H)
    cos_w, sin_w = dft_tables(W)
    window = hann(H, 0, H)[:, None] * hann(W, 0, W)[None, :]

    def forward(tile):
        shaded = (tile * window).astype(jnp.bfloat16)
        y_real = jnp.dot(shaded, cos_w, preferred_element_type=jnp.float32).astype(jnp.bfloat16)
        y_imag = (-jnp.dot(shaded, sin_w, preferred_element_type=jnp.float32)).astype(jnp.bfloat16)
        f_real = jnp.dot(cos_h, y_real, preferred_element_type=jnp.float32) + jnp.dot(sin_h, y_imag, preferred_element_type=jnp.float32)
        f_imag = jnp.dot(cos_h, y_imag, preferred_element_type=jnp.float32) - jnp.dot(sin_h, y_real, preferred_element_type=jnp.float32)
        return jnp.stack([f_real, f_imag]).astype(jnp.bfloat16)
    spectra = lax.map(forward, tiles)

    def one_pair(slot):
        group = slot // PAIR_CAP
        within = slot % PAIR_CAP
        first = pairs[group, within, 0]
        second = pairs[group, within, 1]
        other = (group + N_BLK - N_BLK // 2) % N_BLK
        source = jnp.where(second < TILES_DEV, group, other)
        left = spectra[group * TILES_DEV + first].astype(jnp.float32)
        right = spectra[source * TILES_DEV + second % TILES_DEV].astype(jnp.float32)
        cross_real = left[0] * right[0] + left[1] * right[1]
        cross_imag = left[1] * right[0] - left[0] * right[1]
        factor = 1.0 / (jnp.sqrt(cross_real * cross_real + cross_imag * cross_imag) + FLOOR)
        q_real = (cross_real * factor).astype(jnp.bfloat16)
        q_imag = (cross_imag * factor).astype(jnp.bfloat16)
        z_real = (jnp.dot(cos_h, q_real, preferred_element_type=jnp.float32) - jnp.dot(sin_h, q_imag, preferred_element_type=jnp.float32)).astype(jnp.bfloat16)
        z_imag = (jnp.dot(sin_h, q_real, preferred_element_type=jnp.float32) + jnp.dot(cos_h, q_imag, preferred_element_type=jnp.float32)).astype(jnp.bfloat16)
        surface = jnp.dot(z_real, cos_w, preferred_element_type=jnp.float32) - jnp.dot(z_imag, sin_w, preferred_element_type=jnp.float32)
        live = (within < counts[group]).astype(jnp.float32)
        return surface * live
    return lax.map(one_pair, jnp.arange(N_BLK * PAIR_CAP, dtype=jnp.int32))
```

```python
import functools
import math

import jax
import jax.numpy as jnp
import ml_dtypes
import numpy as np
from jax import lax
from jax.experimental import pallas as pl
from jax.experimental.pallas import tpu as pltpu
from jax.sharding import PartitionSpec as P

FLOOR = 0.05
LANES = 128
MESH = pl.DeviceIdType.MESH
BF16 = jnp.bfloat16
F32 = jnp.float32


def dft_tables(length):
    index = np.arange(length)
    angle = 2.0 * math.pi / length * (index[:, None] * index[None, :] % length)
    factor = 1.0 / math.sqrt(length)
    return (
        (np.cos(angle) * factor).astype(ml_dtypes.bfloat16).astype(np.float32),
        (np.sin(angle) * factor).astype(ml_dtypes.bfloat16).astype(np.float32),
    )


def hann(length):
    return (0.5 - 0.5 * np.cos(2.0 * math.pi / length * np.arange(length))).astype(np.float32)


def row_tables(width, n, width_chunk):
    cos_w, sin_w = dft_tables(width)
    half = width // 2
    real, imag = cos_w[:, :half].copy(), -sin_w[:, :half]
    imag[:, 0] = cos_w[:, half]
    forward = np.stack([real, imag], 1).reshape(width, 2, n, -1, width_chunk).transpose(3, 0, 2, 1, 4)
    inverse_real, inverse_imag = 2.0 * real, 2.0 * imag
    inverse_real[:, 0], inverse_imag[:, 0] = real[:, 0], imag[:, 0]
    inverse = np.stack([inverse_real, inverse_imag], 1).reshape(width, 2, n, -1, width_chunk).transpose(3, 2, 1, 4, 0)
    chunks = half // n // width_chunk
    return (
        forward.reshape(chunks, width, n * 2 * width_chunk).astype(ml_dtypes.bfloat16),
        inverse.reshape(chunks, n * 2 * width_chunk, width).astype(ml_dtypes.bfloat16),
    )


def mm(a, b):
    return jnp.dot(a, b, preferred_element_type=F32)


def kernel(
    n, nb, cw,
    pairs, counts, tiles_hbm, hann_h, hann_w, fwd_hbm, cos_hbm, sin_hbm, inv_hbm,
    out,
    tiles, fwd, cos, sin, inv, shaded, fsend, frecv, ops, spec, pspec, qfix, zsend, zrecv,
    load_sem, fs, fr, zs, zr, bs, br,
):
    me = lax.axis_index("rows")
    blk = lax.axis_index("blk")
    partner = lax.rem(blk + nb // 2, nb)
    groups, band, width = tiles.shape
    height = cos.shape[0]
    chunks = spec.shape[0]
    step = min(256, height // 2)
    steps = height // step
    block = LANES // 2

    loads = [
        pltpu.make_async_copy(src, dst, load_sem.at[i])
        for i, (src, dst) in enumerate(
            [(tiles_hbm, tiles), (fwd_hbm, fwd), (cos_hbm, cos), (sin_hbm, sin), (inv_hbm, inv)]
        )
    ]
    for load in loads:
        load.start()

    barrier = pltpu.get_barrier_semaphore()
    for k in range(1, n):
        pl.semaphore_signal(barrier, inc=1, device_id={"rows": lax.rem(me + k, n)}, device_id_type=MESH)
    pl.semaphore_signal(barrier, inc=1, device_id={"blk": partner}, device_id_type=MESH)

    def lanes_of(rows):
        return lax.broadcasted_iota(jnp.int32, (rows, LANES), 1)

    def is_re_of(rows):
        return lax.rem(lanes_of(rows), 2 * cw) < cw

    def shared_of(rows):
        return lax.rem(lanes_of(rows), cw) == jnp.where(me == 0, 0, -1)

    def swap(x):
        return jnp.where(is_re_of(x.shape[0]), pltpu.roll(x, LANES - cw, 1), pltpu.roll(x, cw, 1))

    def forward_copy(j, k):
        return pltpu.make_async_remote_copy(
            src_ref=fsend.at[j, lax.rem(me + k, n)],
            dst_ref=frecv.at[j, pl.ds(pl.multiple_of(me * band, band), band)],
            send_sem=fs.at[j, k - 1],
            recv_sem=fr.at[j, k - 1],
            device_id={"rows": lax.rem(me + k, n)},
            device_id_type=MESH,
        )

    def partner_copy(j):
        return pltpu.make_async_remote_copy(
            src_ref=spec.at[j],
            dst_ref=pspec.at[j],
            send_sem=zs.at[j],
            recv_sem=zr.at[j],
            device_id={"blk": partner},
            device_id_type=MESH,
        )

    def back_copy(j, k):
        return pltpu.make_async_remote_copy(
            src_ref=zsend.at[j, pl.ds(pl.multiple_of(lax.rem(me + k, n) * band, band), band)],
            dst_ref=zrecv.at[j, me],
            send_sem=bs.at[j, k - 1],
            recv_sem=br.at[j, k - 1],
            device_id={"rows": lax.rem(me + k, n)},
            device_id_type=MESH,
        )

    loads[0].wait()
    for g in range(groups):
        shaded[g] = (tiles[g] * (hann_h[...] * hann_w[...])).astype(BF16)
    loads[1].wait()
    low = lanes_of(band) < block
    for j in range(chunks):
        first = mm(shaded[0], fwd[j])
        second = mm(shaded[1], fwd[j])
        for m in range(n // 2):
            a = first[:, m * LANES : (m + 1) * LANES]
            b = second[:, m * LANES : (m + 1) * LANES]
            fsend[j, 2 * m] = jnp.where(low, a, pltpu.roll(b, block, 1)).astype(BF16)
            fsend[j, 2 * m + 1] = jnp.where(low, pltpu.roll(a, block, 1), b).astype(BF16)
        if j == 0:
            pl.semaphore_wait(barrier, n)
        for k in range(1, n):
            forward_copy(j, k).start()
        frecv[j, pl.ds(pl.multiple_of(me * band, band), band)] = fsend[j, me]

    loads[2].wait()
    loads[3].wait()
    for j in range(chunks):
        for k in range(1, n):
            forward_copy(j, k).wait_recv()
        for half in range(2 if j == 0 else 1):

            def operands(i, _, half=half, j=j):
                at = pl.ds(pl.multiple_of(i * step, step), step)
                y = frecv[j, at].astype(F32)
                is_re, shared = is_re_of(step), shared_of(step)
                if j == 0:
                    y = jnp.where(shared, jnp.where(is_re, swap(y) if half else y, 0.0), y)
                other = swap(y)
                ops[half, 0, at] = y.astype(BF16)
                ops[half, 1, at] = jnp.where(is_re, other, -other).astype(BF16)
                return 0

            lax.fori_loop(0, steps, operands, 0)
        for half in range(2):
            use = half if j == 0 else 0

            def columns(i, _, use=use, j=j):
                at = pl.ds(pl.multiple_of(i * step, step), step)
                spec[j, at] = (mm(cos[at], ops[use, 0]) + mm(sin[at], ops[use, 1])).astype(BF16)
                return 0

            lax.fori_loop(half * steps // 2, (half + 1) * steps // 2, columns, 0)
        if j == 0:
            middle = height // 2
            rows = lax.broadcasted_iota(jnp.int32, (16, LANES), 0)
            mark = (rows == 0) & shared_of(16) & ~is_re_of(16)
            top = swap(mm(cos[middle : middle + 16], ops[0, 0]))
            bottom = swap(mm(cos[0:16], ops[1, 0]))
            spec[0, 0:16] = jnp.where(mark, top, spec[0, 0:16].astype(F32)).astype(BF16)
            spec[0, middle : middle + 16] = jnp.where(
                mark, bottom, spec[0, middle : middle + 16].astype(F32)
            ).astype(BF16)
        partner_copy(j).start()

    def gather(j):
        for k in range(1, n):
            back_copy(j, k).wait_recv()
        parts = [[], []]
        for m in range(n // 2):
            a = zrecv[j, 2 * m].astype(F32)
            b = zrecv[j, 2 * m + 1].astype(F32)
            parts[0].append(jnp.where(low, a, pltpu.roll(b, block, 1)).astype(BF16))
            parts[1].append(jnp.where(low, pltpu.roll(a, block, 1), b).astype(BF16))
        for p in range(2):
            z = jnp.concatenate(parts[p], axis=1)
            scale = jnp.where(p < counts[0], 1.0, 0.0).astype(F32)
            for c in range(0, width, 256):
                value = mm(z, inv[j, :, c : c + 256])
                if j > 0:
                    value = out[p, :, c : c + 256] + value
                if j == chunks - 1:
                    value = value * scale
                out[p, :, c : c + 256] = value

    for j in range(chunks):
        partner_copy(j).wait_recv()

        def cross(i, _, j=j, bottom=False):
            at = pl.ds(pl.multiple_of(i * step, step), step)
            is_re = is_re_of(step)
            slot_low = lanes_of(step) < block
            own = spec[j, at].astype(F32)
            far = pspec[j, at].astype(F32)
            own_turned = pltpu.roll(own, block, 1)
            far_turned = pltpu.roll(far, block, 1)
            want_left = jnp.where(slot_low, pairs[0], 1 - pairs[2])
            want_right = jnp.where(slot_low, lax.rem(pairs[1], 2), 1 - lax.rem(pairs[3], 2))
            want_far = jnp.where(slot_low, pairs[1], pairs[3]) >= 2
            left = jnp.where(want_left == 0, own, own_turned)
            right = jnp.where(
                want_right == 0, jnp.where(want_far, far, own), jnp.where(want_far, far_turned, own_turned)
            )
            left_other, right_other = swap(left), swap(right)
            crossed = jnp.where(
                is_re, left * right + left_other * right_other, left * right_other - left_other * right
            )
            crossed_other = swap(crossed)
            power = crossed * crossed + crossed_other * crossed_other
            if j == 0:
                shared = shared_of(step)
                rows = lax.broadcasted_iota(jnp.int32, (step, LANES), 0) + i * step
                single = shared & (lax.rem(rows, height // 2) == 0)
                crossed = jnp.where(single, left * right, crossed)
                power = jnp.where(single, crossed * crossed, power)
            q = (crossed / (jnp.sqrt(power) + FLOOR)).astype(BF16).astype(F32)
            other = swap(q)
            for_cos, for_sin = q, jnp.where(is_re, -other, other)
            if j == 0:
                weight = jnp.where(single, 1.0, 2.0)
                if bottom:
                    for_cos = jnp.where(shared, jnp.where(is_re, 0.0, weight * other), for_cos)
                    for_sin = jnp.where(shared, jnp.where(is_re, 0.0, -2.0 * q), for_sin)
                else:
                    for_cos = jnp.where(shared, jnp.where(is_re, weight * q, 0.0), for_cos)
                    for_sin = jnp.where(shared, jnp.where(is_re, -2.0 * other, 0.0), for_sin)

                @pl.when(lax.rem(i, steps // 2) == 0)
                def _():
                    qfix[1 if bottom else 0] = q[0:16]

            ops[0, 0, at] = for_cos.astype(BF16)
            ops[0, 1, at] = for_sin.astype(BF16)
            return 0

        lax.fori_loop(0, steps // 2, functools.partial(cross, bottom=False), 0)
        lax.fori_loop(steps // 2, steps, functools.partial(cross, bottom=True), 0)
        if j == 0:
            middle = height // 2
            rows = lax.broadcasted_iota(jnp.int32, (16, LANES), 0)
            mark = (rows == 0) & shared_of(16)
            is_re = is_re_of(16)
            ops[0, 0, 0:16] = jnp.where(mark & ~is_re, qfix[1], ops[0, 0, 0:16].astype(F32)).astype(BF16)
            ops[0, 0, middle : middle + 16] = jnp.where(
                mark & is_re, swap(qfix[0]), ops[0, 0, middle : middle + 16].astype(F32)
            ).astype(BF16)

        def inverse(i, _, j=j):
            at = pl.ds(pl.multiple_of(i * step, step), step)
            zsend[j, at] = (mm(cos[at], ops[0, 0]) + mm(sin[at], ops[0, 1])).astype(BF16)
            return 0

        lax.fori_loop(0, steps, inverse, 0)
        for k in range(1, n):
            back_copy(j, k).start()
        zrecv[j, me] = zsend[j, pl.ds(pl.multiple_of(me * band, band), band)]
        if j == 0:
            loads[4].wait()
        else:
            gather(j - 1)
    gather(chunks - 1)

    for j in range(chunks):
        for k in range(1, n):
            forward_copy(j, k).wait_send()
            back_copy(j, k).wait_send()
        partner_copy(j).wait_send()


def local(tiles, pairs, counts):
    n = lax.axis_size("rows")
    nb = lax.axis_size("blk")
    groups, band, width = tiles.shape
    slots = pairs.shape[1]
    height = band * n
    cw = LANES // (2 * groups)
    chunks = width // 2 // n // cw
    cos_h, sin_h = dft_tables(height)
    forward, inverse = row_tables(width, n, cw)
    rows = lax.dynamic_slice(jnp.asarray(hann(height)), (lax.axis_index("rows") * band,), (band,))
    vmem = pl.BlockSpec(memory_space=pltpu.VMEM)
    smem = pl.BlockSpec(memory_space=pltpu.SMEM)
    hbm = pl.BlockSpec(memory_space=pl.ANY)
    dma = pltpu.SemaphoreType.DMA
    return pl.pallas_call(
        functools.partial(kernel, n, nb, cw),
        out_shape=jax.ShapeDtypeStruct((slots, band, width), F32),
        in_specs=[smem, smem, hbm, vmem, vmem, hbm, hbm, hbm, hbm],
        out_specs=vmem,
        scratch_shapes=[
            pltpu.VMEM(tiles.shape, F32),
            pltpu.VMEM(forward.shape, BF16),
            pltpu.VMEM((height, height), BF16),
            pltpu.VMEM((height, height), BF16),
            pltpu.VMEM(inverse.shape, BF16),
            pltpu.VMEM(tiles.shape, BF16),
            pltpu.VMEM((chunks, n, band, LANES), BF16),
            pltpu.VMEM((chunks, height, LANES), BF16),
            pltpu.VMEM((2, 2, height, LANES), BF16),
            pltpu.VMEM((chunks, height, LANES), BF16),
            pltpu.VMEM((chunks, height, LANES), BF16),
            pltpu.VMEM((2, 16, LANES), F32),
            pltpu.VMEM((chunks, height, LANES), BF16),
            pltpu.VMEM((chunks, n, band, LANES), BF16),
            dma((5,)),
            dma((chunks, n - 1)),
            dma((chunks, n - 1)),
            dma((chunks,)),
            dma((chunks,)),
            dma((chunks, n - 1)),
            dma((chunks, n - 1)),
        ],
        compiler_params=pltpu.CompilerParams(
            collective_id=0, has_side_effects=True, vmem_limit_bytes=48 * 1024 * 1024
        ),
    )(
        pairs.reshape(-1),
        counts,
        tiles,
        rows[:, None],
        jnp.asarray(hann(width))[None, :],
        jnp.asarray(forward),
        jnp.asarray(cos_h.astype(ml_dtypes.bfloat16)),
        jnp.asarray(sin_h.astype(ml_dtypes.bfloat16)),
        jnp.asarray(inverse),
    )


def solution(mesh):
    return jax.shard_map(
        local,
        mesh=mesh,
        in_specs=(
            P(("parts", "blk"), "rows", None),
            P(("parts", "blk"), None, None),
            P(("parts", "blk")),
        ),
        out_specs=P(("parts", "blk"), "rows", None),
        check_vma=False,
    )
```

```python
import functools
import math

import jax
import jax.numpy as jnp
import ml_dtypes
import numpy as np
from jax import lax
from jax.experimental import pallas as pl
from jax.experimental.pallas import tpu as pltpu
from jax.sharding import PartitionSpec as P

FLOOR = 0.05
LANES = 128
MESH = pl.DeviceIdType.MESH
BF16 = jnp.bfloat16
F32 = jnp.float32


def dft_tables(length):
    index = np.arange(length)
    angle = 2.0 * math.pi / length * (index[:, None] * index[None, :] % length)
    factor = 1.0 / math.sqrt(length)
    return (
        (np.cos(angle) * factor).astype(ml_dtypes.bfloat16).astype(np.float32),
        (np.sin(angle) * factor).astype(ml_dtypes.bfloat16).astype(np.float32),
    )


def hann(length):
    return (0.5 - 0.5 * np.cos(2.0 * math.pi / length * np.arange(length))).astype(np.float32)


def row_tables(width, n, width_chunk):
    cos_w, sin_w = dft_tables(width)
    half = width // 2
    real, imag = cos_w[:, :half].copy(), -sin_w[:, :half]
    imag[:, 0] = cos_w[:, half]
    forward = np.stack([real, imag], 1).reshape(width, 2, n, -1, width_chunk).transpose(3, 0, 2, 1, 4)
    inverse_real, inverse_imag = 2.0 * real, 2.0 * imag
    inverse_real[:, 0], inverse_imag[:, 0] = real[:, 0], imag[:, 0]
    inverse = np.stack([inverse_real, inverse_imag], 1).reshape(width, 2, n, -1, width_chunk).transpose(3, 2, 1, 4, 0)
    chunks = half // n // width_chunk
    return (
        forward.reshape(chunks, width, n * 2 * width_chunk).astype(ml_dtypes.bfloat16),
        inverse.reshape(chunks, n * 2 * width_chunk, width).astype(ml_dtypes.bfloat16),
    )


def mm(a, b):
    return jnp.dot(a, b, preferred_element_type=F32)


def kernel(
    n, nb, cw,
    pairs, counts, tiles_hbm, hann_hbm, hann_w, fwd_hbm, cos_hbm, sin_hbm, inv_hbm,
    out_hbm,
    out, tiles, hann_h, fwd, cos, sin, inv, shaded, fsend, frecv, far, ops, spec, pspec, qfix, zsum, zsend, zrecv,
    load_sem, out_sem, fs, fr, gs, gr, zs, zr, bs, br,
):
    me = lax.axis_index("rows")
    blk = lax.axis_index("blk")
    partner = lax.rem(blk + nb // 2, nb)
    groups, band, width = tiles.shape
    height = cos.shape[0]
    chunks = spec.shape[0]
    step = min(256, height // 2)
    steps = height // step
    block = LANES // 2
    middle = height // 2
    order = [n // 2] + [k for k in range(1, n) if k != n // 2]

    loads = [
        pltpu.make_async_copy(src, dst, load_sem.at[i])
        for i, (src, dst) in enumerate(
            [(tiles_hbm, tiles), (hann_hbm.at[me], hann_h), (fwd_hbm, fwd), (cos_hbm, cos), (sin_hbm, sin), (inv_hbm, inv)]
        )
    ]
    for load in loads:
        load.start()

    barrier = pltpu.get_barrier_semaphore()
    for k in range(1, n):
        pl.semaphore_signal(barrier, inc=1, device_id={"rows": lax.rem(me + k, n)}, device_id_type=MESH)
    for k in range(n):
        pl.semaphore_signal(
            barrier, inc=1, device_id={"blk": partner, "rows": lax.rem(me + k, n)}, device_id_type=MESH
        )

    def lanes_of(rows):
        return lax.broadcasted_iota(jnp.int32, (rows, LANES), 1)

    def is_re_of(rows):
        return lax.rem(lanes_of(rows), 2 * cw) < cw

    def shared_of(rows):
        return lax.rem(lanes_of(rows), cw) == jnp.where(me == 0, 0, -1)

    def swap(x):
        return jnp.where(is_re_of(x.shape[0]), pltpu.roll(x, LANES - cw, 1), pltpu.roll(x, cw, 1))

    def forward_copy(j, k):
        return pltpu.make_async_remote_copy(
            src_ref=fsend.at[j, lax.rem(me + k, n)],
            dst_ref=frecv.at[j, pl.ds(pl.multiple_of(me * band, band), band)],
            send_sem=fs.at[j, k - 1],
            recv_sem=fr.at[j, k - 1],
            device_id={"rows": lax.rem(me + k, n)},
            device_id_type=MESH,
        )

    def far_copy(k):
        return pltpu.make_async_remote_copy(
            src_ref=fsend.at[0, lax.rem(me + k, n)],
            dst_ref=far.at[pl.ds(pl.multiple_of(me * band, band), band)],
            send_sem=gs.at[k],
            recv_sem=gr.at[k],
            device_id={"blk": partner, "rows": lax.rem(me + k, n)},
            device_id_type=MESH,
        )

    def partner_copy(j, half):
        at = pl.ds(half * middle, middle)
        return pltpu.make_async_remote_copy(
            src_ref=spec.at[j, at],
            dst_ref=pspec.at[j, at],
            send_sem=zs.at[j, half],
            recv_sem=zr.at[j, half],
            device_id={"blk": partner},
            device_id_type=MESH,
        )

    def store(p):
        return pltpu.make_async_copy(out.at[p], out_hbm.at[p], out_sem.at[p])

    def back_copy(j, k):
        return pltpu.make_async_remote_copy(
            src_ref=zsend.at[j, pl.ds(pl.multiple_of(lax.rem(me + k, n) * band, band), band)],
            dst_ref=zrecv.at[j, me],
            send_sem=bs.at[j, k - 1],
            recv_sem=br.at[j, k - 1],
            device_id={"rows": lax.rem(me + k, n)},
            device_id_type=MESH,
        )

    loads[0].wait()
    loads[1].wait()
    for g in range(groups):
        shaded[g] = (tiles[g] * (hann_h[:, 0:1] * hann_w[...])).astype(BF16)
    loads[2].wait()
    low = lanes_of(band) < block

    def rows_to_columns(j):
        first = mm(shaded[0], fwd[j])
        second = mm(shaded[1], fwd[j])
        for m in range(n // 2):
            a = first[:, m * LANES : (m + 1) * LANES]
            b = second[:, m * LANES : (m + 1) * LANES]
            fsend[j, 2 * m] = jnp.where(low, a, pltpu.roll(b, block, 1)).astype(BF16)
            fsend[j, 2 * m + 1] = jnp.where(low, pltpu.roll(a, block, 1), b).astype(BF16)
        frecv[j, pl.ds(pl.multiple_of(me * band, band), band)] = fsend[j, me]

    def transform(source, target, shares):
        for half in range(2 if shares else 1):

            def operands(i, _, half=half):
                at = pl.ds(pl.multiple_of(i * step, step), step)
                y = source[at].astype(F32)
                is_re = is_re_of(step)
                if shares:
                    y = jnp.where(shared_of(step), jnp.where(is_re, swap(y) if half else y, 0.0), y)
                other = swap(y)
                ops[half, 0, at] = y.astype(BF16)
                ops[half, 1, at] = jnp.where(is_re, other, -other).astype(BF16)
                return 0

            lax.fori_loop(0, steps, operands, 0)
        for half in range(2):
            use = half if shares else 0

            def columns(i, _, use=use):
                at = pl.ds(pl.multiple_of(i * step, step), step)
                target[at] = (mm(cos[at], ops[use, 0]) + mm(sin[at], ops[use, 1])).astype(BF16)
                return 0

            lax.fori_loop(half * steps // 2, (half + 1) * steps // 2, columns, 0)
        if shares:
            rows = lax.broadcasted_iota(jnp.int32, (16, LANES), 0)
            mark = (rows == 0) & shared_of(16) & ~is_re_of(16)
            top = swap(mm(cos[middle : middle + 16], ops[0, 0]))
            bottom = swap(mm(cos[0:16], ops[1, 0]))
            target[0:16] = jnp.where(mark, top, target[0:16].astype(F32)).astype(BF16)
            target[middle : middle + 16] = jnp.where(
                mark, bottom, target[middle : middle + 16].astype(F32)
            ).astype(BF16)

    rows_to_columns(0)
    pl.semaphore_wait(barrier, 2 * n - 1)
    for k in order:
        forward_copy(0, k).start()
    for k in range(n):
        far_copy(k).start()
    for j in range(chunks):
        if j + 1 < chunks:
            rows_to_columns(j + 1)
        for k in range(1, n):
            forward_copy(j, k).wait_recv()
        if j + 1 < chunks:
            for k in order:
                forward_copy(j + 1, k).start()
        if j == 0:
            loads[3].wait()
            loads[4].wait()
        transform(frecv.at[j], spec.at[j], j == 0)
        if j == 1:
            for half in range(2):
                partner_copy(j, half).start()

    def gather(j):
        for k in range(1, n):
            back_copy(j, k).wait_recv()
        parts = [[], []]
        for m in range(n // 2):
            a = zrecv[j, 2 * m].astype(F32)
            b = zrecv[j, 2 * m + 1].astype(F32)
            parts[0].append(jnp.where(low, a, pltpu.roll(b, block, 1)).astype(BF16))
            parts[1].append(jnp.where(low, pltpu.roll(a, block, 1), b).astype(BF16))
        for p in range(2):
            z = jnp.concatenate(parts[p], axis=1)
            scale = jnp.where(p < counts[0], 1.0, 0.0).astype(F32)
            for c in range(0, width, 256):
                value = mm(z, inv[j, :, c : c + 256])
                if j > 0:
                    value = out[p, :, c : c + 256] + value
                if j == chunks - 1:
                    value = value * scale
                out[p, :, c : c + 256] = value
            if j == chunks - 1:
                store(p).start()

    for j in range(chunks):
        if j == 0:
            for k in range(n):
                far_copy(k).wait_recv()
        else:
            partner_copy(j, 0).wait_recv()
            if j < chunks - 1:
                partner_copy(j, 1).wait_recv()
        if j + 2 < chunks:
            for half in range(2):
                partner_copy(j + 2, half).start()
        if j == 0:
            transform(far, pspec.at[0], True)

        def cross(i, _, j=j, bottom=False):
            at = pl.ds(pl.multiple_of(i * step, step), step)
            is_re = is_re_of(step)
            slot_low = lanes_of(step) < block
            own = spec[j, at].astype(F32)
            far = pspec[j, at].astype(F32)
            own_turned = pltpu.roll(own, block, 1)
            far_turned = pltpu.roll(far, block, 1)
            want_left = jnp.where(slot_low, pairs[0, 0, 0], 1 - pairs[0, 1, 0])
            want_right = jnp.where(slot_low, lax.rem(pairs[0, 0, 1], 2), 1 - lax.rem(pairs[0, 1, 1], 2))
            want_far = jnp.where(slot_low, pairs[0, 0, 1], pairs[0, 1, 1]) >= 2
            left = jnp.where(want_left == 0, own, own_turned)
            right = jnp.where(
                want_right == 0, jnp.where(want_far, far, own), jnp.where(want_far, far_turned, own_turned)
            )
            left_other, right_other = swap(left), swap(right)
            crossed = jnp.where(
                is_re, left * right + left_other * right_other, left * right_other - left_other * right
            )
            crossed_other = swap(crossed)
            power = crossed * crossed + crossed_other * crossed_other
            if j == 0:
                shared = shared_of(step)
                rows = lax.broadcasted_iota(jnp.int32, (step, LANES), 0) + i * step
                single = shared & (lax.rem(rows, height // 2) == 0)
                crossed = jnp.where(single, left * right, crossed)
                power = jnp.where(single, crossed * crossed, power)
            q = (crossed / (jnp.sqrt(power) + FLOOR)).astype(BF16).astype(F32)
            other = swap(q)
            for_cos, for_sin = q, jnp.where(is_re, -other, other)
            if j == 0:
                weight = jnp.where(single, 1.0, 2.0)
                if bottom:
                    for_cos = jnp.where(shared, jnp.where(is_re, 0.0, weight * other), for_cos)
                    for_sin = jnp.where(shared, jnp.where(is_re, 0.0, -2.0 * q), for_sin)
                else:
                    for_cos = jnp.where(shared, jnp.where(is_re, weight * q, 0.0), for_cos)
                    for_sin = jnp.where(shared, jnp.where(is_re, -2.0 * other, 0.0), for_sin)

                @pl.when(lax.rem(i, steps // 2) == 0)
                def _():
                    qfix[1 if bottom else 0] = q[0:16]

            ops[0, 0, at] = for_cos.astype(BF16)
            ops[0, 1, at] = for_sin.astype(BF16)
            return 0

        lax.fori_loop(0, steps // 2, functools.partial(cross, bottom=False), 0)
        split = 0 < j == chunks - 1
        if split:

            def part(i, _):
                at = pl.ds(pl.multiple_of(i * step, step), step)
                zsum[at] = mm(cos[at, 0:middle], ops[0, 0, 0:middle]) + mm(sin[at, 0:middle], ops[0, 1, 0:middle])
                return 0

            lax.fori_loop(0, steps, part, 0)
            partner_copy(j, 1).wait_recv()
        lax.fori_loop(steps // 2, steps, functools.partial(cross, bottom=True), 0)
        if j == 0:
            rows = lax.broadcasted_iota(jnp.int32, (16, LANES), 0)
            mark = (rows == 0) & shared_of(16)
            is_re = is_re_of(16)
            ops[0, 0, 0:16] = jnp.where(mark & ~is_re, qfix[1], ops[0, 0, 0:16].astype(F32)).astype(BF16)
            ops[0, 0, middle : middle + 16] = jnp.where(
                mark & is_re, swap(qfix[0]), ops[0, 0, middle : middle + 16].astype(F32)
            ).astype(BF16)
        for k in order + [0]:
            at = pl.ds(pl.multiple_of(lax.rem(me + k, n) * band, band), band)
            if split:
                z = mm(cos[at, middle:], ops[0, 0, middle:]) + mm(sin[at, middle:], ops[0, 1, middle:]) + zsum[at]
            else:
                z = mm(cos[at], ops[0, 0]) + mm(sin[at], ops[0, 1])
            if k:
                zsend[j, at] = z.astype(BF16)
                back_copy(j, k).start()
            else:
                zrecv[j, me] = z.astype(BF16)
        if j == 0:
            loads[5].wait()
        else:
            gather(j - 1)
    gather(chunks - 1)

    for j in range(chunks):
        for k in range(1, n):
            forward_copy(j, k).wait_send()
            back_copy(j, k).wait_send()
        if j > 0:
            for half in range(2):
                partner_copy(j, half).wait_send()
    for k in range(n):
        far_copy(k).wait_send()
    for p in range(2):
        store(p).wait()


def local(tiles, pairs, counts):
    n = lax.axis_size("rows")
    nb = lax.axis_size("blk")
    groups, band, width = tiles.shape
    slots = pairs.shape[1]
    height = band * n
    cw = LANES // (2 * groups)
    chunks = width // 2 // n // cw
    cos_h, sin_h = dft_tables(height)
    forward, inverse = row_tables(width, n, cw)
    hann_h = np.repeat(hann(height).reshape(n, band, 1), LANES, axis=2)
    vmem = pl.BlockSpec(memory_space=pltpu.VMEM)
    smem = pl.BlockSpec(memory_space=pltpu.SMEM)
    hbm = pl.BlockSpec(memory_space=pltpu.HBM)
    dma = pltpu.SemaphoreType.DMA
    return pl.pallas_call(
        functools.partial(kernel, n, nb, cw),
        out_shape=jax.ShapeDtypeStruct((slots, band, width), F32),
        in_specs=[smem, smem, hbm, hbm, vmem, hbm, hbm, hbm, hbm],
        out_specs=hbm,
        scratch_shapes=[
            pltpu.VMEM((slots, band, width), F32),
            pltpu.VMEM(tiles.shape, F32),
            pltpu.VMEM((band, LANES), F32),
            pltpu.VMEM(forward.shape, BF16),
            pltpu.VMEM((height, height), BF16),
            pltpu.VMEM((height, height), BF16),
            pltpu.VMEM(inverse.shape, BF16),
            pltpu.VMEM(tiles.shape, BF16),
            pltpu.VMEM((chunks, n, band, LANES), BF16),
            pltpu.VMEM((chunks, height, LANES), BF16),
            pltpu.VMEM((height, LANES), BF16),
            pltpu.VMEM((2, 2, height, LANES), BF16),
            pltpu.VMEM((chunks, height, LANES), BF16),
            pltpu.VMEM((chunks, height, LANES), BF16),
            pltpu.VMEM((2, 16, LANES), F32),
            pltpu.VMEM((height, LANES), F32),
            pltpu.VMEM((chunks, height, LANES), BF16),
            pltpu.VMEM((chunks, n, band, LANES), BF16),
            dma((6,)),
            dma((slots,)),
            dma((chunks, n - 1)),
            dma((chunks, n - 1)),
            dma((n,)),
            dma((n,)),
            dma((chunks, 2)),
            dma((chunks, 2)),
            dma((chunks, n - 1)),
            dma((chunks, n - 1)),
        ],
        compiler_params=pltpu.CompilerParams(
            collective_id=0, has_side_effects=True, vmem_limit_bytes=56 * 1024 * 1024
        ),
    )(
        pairs,
        counts,
        tiles,
        jnp.asarray(hann_h),
        jnp.asarray(hann(width))[None, :],
        jnp.asarray(forward),
        jnp.asarray(cos_h.astype(ml_dtypes.bfloat16)),
        jnp.asarray(sin_h.astype(ml_dtypes.bfloat16)),
        jnp.asarray(inverse),
    )


def solution(mesh):
    return jax.shard_map(
        local,
        mesh=mesh,
        in_specs=(
            P(("parts", "blk"), "rows", None),
            P(("parts", "blk"), None, None),
            P(("parts", "blk")),
        ),
        out_specs=P(("parts", "blk"), "rows", None),
        check_vma=False,
    )
```

```python
import functools
import math

import jax
import jax.numpy as jnp
import ml_dtypes
import numpy as np
from jax import lax
from jax.experimental import pallas as pl
from jax.experimental.pallas import tpu as pltpu
from jax.sharding import PartitionSpec as P

FLOOR = 0.05
LANES = 128
MESH = pl.DeviceIdType.MESH
BF16 = jnp.bfloat16
F32 = jnp.float32


def dft_tables(length):
    index = np.arange(length)
    angle = 2.0 * math.pi / length * (index[:, None] * index[None, :] % length)
    factor = 1.0 / math.sqrt(length)
    return (
        (np.cos(angle) * factor).astype(ml_dtypes.bfloat16).astype(np.float32),
        (np.sin(angle) * factor).astype(ml_dtypes.bfloat16).astype(np.float32),
    )


def hann(length):
    return (0.5 - 0.5 * np.cos(2.0 * math.pi / length * np.arange(length))).astype(np.float32)


def row_tables(width, n, width_chunk):
    cos_w, sin_w = dft_tables(width)
    half = width // 2
    real, imag = cos_w[:, :half].copy(), -sin_w[:, :half]
    imag[:, 0] = cos_w[:, half]
    forward = np.stack([real, imag], 1).reshape(width, 2, n, -1, width_chunk).transpose(3, 0, 2, 1, 4)
    inverse_real, inverse_imag = 2.0 * real, 2.0 * imag
    inverse_real[:, 0], inverse_imag[:, 0] = real[:, 0], imag[:, 0]
    inverse = np.stack([inverse_real, inverse_imag], 1).reshape(width, 2, n, -1, width_chunk).transpose(3, 2, 1, 4, 0)
    chunks = half // n // width_chunk
    return (
        forward.reshape(chunks, width, n * 2 * width_chunk).astype(ml_dtypes.bfloat16),
        inverse.reshape(chunks, n * 2 * width_chunk, width).astype(ml_dtypes.bfloat16),
    )


def mm(a, b):
    return jnp.dot(a, b, preferred_element_type=F32)


def kernel(
    n, nb, cw,
    pairs, counts, tiles_hbm, hann_hbm, hann_w, fwd_hbm, cos_hbm, sin_hbm, inv_hbm,
    out,
    tiles, hann_h, fwd, cos, sin, inv, shaded, fsend, frecv, far, ops, spec, pspec, qfix, zsum, zsend, zrecv,
    load_sem, fs, fr, gs, gr, zs, zr, bs, br,
):
    me = lax.axis_index("rows")
    blk = lax.axis_index("blk")
    partner = lax.rem(blk + nb // 2, nb)
    groups, band, width = tiles.shape
    height = cos.shape[0]
    chunks = spec.shape[0]
    step = min(256, height // 4)
    steps = height // step
    block = LANES // 2
    middle = height // 2
    parts = zs.shape[1]
    order = [n // 2] + [k for k in range(1, n) if k != n // 2]

    loads = [
        pltpu.make_async_copy(src, dst, load_sem.at[i])
        for i, (src, dst) in enumerate(
            [
                (tiles_hbm, tiles),
                (hann_hbm.at[me], hann_h),
                (fwd_hbm.at[0], fwd.at[0]),
                (fwd_hbm.at[pl.ds(1, chunks - 1)], fwd.at[pl.ds(1, chunks - 1)]),
                (cos_hbm, cos),
                (sin_hbm, sin),
                (inv_hbm, inv),
            ]
        )
    ]
    for load in loads[:3]:
        load.start()

    barrier = pltpu.get_barrier_semaphore()
    for k in range(1, n):
        pl.semaphore_signal(barrier, inc=1, device_id={"rows": lax.rem(me + k, n)}, device_id_type=MESH)
    for k in range(n):
        pl.semaphore_signal(
            barrier, inc=1, device_id={"blk": partner, "rows": lax.rem(me + k, n)}, device_id_type=MESH
        )

    def lanes_of(rows):
        return lax.broadcasted_iota(jnp.int32, (rows, LANES), 1)

    def is_re_of(rows):
        return lax.rem(lanes_of(rows), 2 * cw) < cw

    def shared_of(rows):
        return lax.rem(lanes_of(rows), cw) == jnp.where(me == 0, 0, -1)

    def swap(x):
        return jnp.where(is_re_of(x.shape[0]), pltpu.roll(x, LANES - cw, 1), pltpu.roll(x, cw, 1))

    def forward_copy(j, k):
        return pltpu.make_async_remote_copy(
            src_ref=fsend.at[j, lax.rem(me + k, n)],
            dst_ref=frecv.at[j, pl.ds(pl.multiple_of(me * band, band), band)],
            send_sem=fs.at[j, k - 1],
            recv_sem=fr.at[j, k - 1],
            device_id={"rows": lax.rem(me + k, n)},
            device_id_type=MESH,
        )

    def far_copy(k):
        return pltpu.make_async_remote_copy(
            src_ref=fsend.at[0, lax.rem(me + k, n)],
            dst_ref=far.at[pl.ds(pl.multiple_of(me * band, band), band)],
            send_sem=gs.at[k],
            recv_sem=gr.at[k],
            device_id={"blk": partner, "rows": lax.rem(me + k, n)},
            device_id_type=MESH,
        )

    def partner_copy(j, part):
        at = pl.ds(part * (height // parts), height // parts)
        return pltpu.make_async_remote_copy(
            src_ref=spec.at[j, at],
            dst_ref=pspec.at[j, at],
            send_sem=zs.at[j, part],
            recv_sem=zr.at[j, part],
            device_id={"blk": partner},
            device_id_type=MESH,
        )

    def back_copy(j, k):
        return pltpu.make_async_remote_copy(
            src_ref=zsend.at[j, pl.ds(pl.multiple_of(lax.rem(me + k, n) * band, band), band)],
            dst_ref=zrecv.at[j, me],
            send_sem=bs.at[j, k - 1],
            recv_sem=br.at[j, k - 1],
            device_id={"rows": lax.rem(me + k, n)},
            device_id_type=MESH,
        )

    loads[0].wait()
    loads[1].wait()
    for g in range(groups):
        shaded[g] = (tiles[g] * (hann_h[:, 0:1] * hann_w[...])).astype(BF16)
    loads[2].wait()
    for load in loads[3:6]:
        load.start()
    low = lanes_of(band) < block

    def rows_to_columns(j):
        first = mm(shaded[0], fwd[j])
        second = mm(shaded[1], fwd[j])
        for m in range(n // 2):
            a = first[:, m * LANES : (m + 1) * LANES]
            b = second[:, m * LANES : (m + 1) * LANES]
            fsend[j, 2 * m] = jnp.where(low, a, pltpu.roll(b, block, 1)).astype(BF16)
            fsend[j, 2 * m + 1] = jnp.where(low, pltpu.roll(a, block, 1), b).astype(BF16)
        frecv[j, pl.ds(pl.multiple_of(me * band, band), band)] = fsend[j, me]

    def transform(source, target, shares):
        for half in range(2 if shares else 1):

            def operands(i, _, half=half):
                at = pl.ds(pl.multiple_of(i * step, step), step)
                y = source[at].astype(F32)
                is_re = is_re_of(step)
                if shares:
                    y = jnp.where(shared_of(step), jnp.where(is_re, swap(y) if half else y, 0.0), y)
                other = swap(y)
                ops[half, 0, at] = y.astype(BF16)
                ops[half, 1, at] = jnp.where(is_re, other, -other).astype(BF16)
                return 0

            lax.fori_loop(0, steps, operands, 0)
        for half in range(2):
            use = half if shares else 0

            def columns(i, _, use=use):
                at = pl.ds(pl.multiple_of(i * step, step), step)
                target[at] = (mm(cos[at], ops[use, 0]) + mm(sin[at], ops[use, 1])).astype(BF16)
                return 0

            lax.fori_loop(half * steps // 2, (half + 1) * steps // 2, columns, 0)
        if shares:
            rows = lax.broadcasted_iota(jnp.int32, (16, LANES), 0)
            mark = (rows == 0) & shared_of(16) & ~is_re_of(16)
            top = swap(mm(cos[middle : middle + 16], ops[0, 0]))
            bottom = swap(mm(cos[0:16], ops[1, 0]))
            target[0:16] = jnp.where(mark, top, target[0:16].astype(F32)).astype(BF16)
            target[middle : middle + 16] = jnp.where(
                mark, bottom, target[middle : middle + 16].astype(F32)
            ).astype(BF16)

    rows_to_columns(0)
    pl.semaphore_wait(barrier, 2 * n - 1)
    for k in range(n):
        far_copy(k).start()
    loads[3].wait()
    turns = [1, 0] + list(range(2, chunks))
    rows_to_columns(turns[0])
    for k in order:
        forward_copy(turns[0], k).start()
    for at, j in enumerate(turns):
        later = turns[at + 1] if at + 1 < chunks else None
        if later:
            rows_to_columns(later)
        for k in range(1, n):
            forward_copy(j, k).wait_recv()
        if later is not None:
            for k in order:
                forward_copy(later, k).start()
        if at == 0:
            loads[4].wait()
            loads[5].wait()
            loads[6].start()
        transform(frecv.at[j], spec.at[j], j == 0)
        if j == 1:
            for part in range(parts):
                partner_copy(j, part).start()

    def gather(j):
        for k in range(1, n):
            back_copy(j, k).wait_recv()
        slabs = [[], []]
        for m in range(n // 2):
            a = zrecv[j, 2 * m].astype(F32)
            b = zrecv[j, 2 * m + 1].astype(F32)
            slabs[0].append(jnp.where(low, a, pltpu.roll(b, block, 1)).astype(BF16))
            slabs[1].append(jnp.where(low, pltpu.roll(a, block, 1), b).astype(BF16))
        for p in range(2):
            z = jnp.concatenate(slabs[p], axis=1)
            scale = jnp.where(p < counts[0], 1.0, 0.0).astype(F32)
            for c in range(0, width, 256):
                value = mm(z, inv[j, :, c : c + 256])
                if j > 0:
                    value = out[p, :, c : c + 256] + value
                if j == chunks - 1:
                    value = value * scale
                out[p, :, c : c + 256] = value

    for j in range(chunks):
        if j == 0:
            for k in range(n):
                far_copy(k).wait_recv()
        else:
            for part in range(parts if j < chunks - 1 else 1):
                partner_copy(j, part).wait_recv()
        if j + 2 < chunks:
            for part in range(parts):
                partner_copy(j + 2, part).start()
        if j == 0:
            transform(far, pspec.at[0], True)

        def cross(i, _, j=j, bottom=False):
            at = pl.ds(pl.multiple_of(i * step, step), step)
            is_re = is_re_of(step)
            slot_low = lanes_of(step) < block
            own = spec[j, at].astype(F32)
            far = pspec[j, at].astype(F32)
            own_turned = pltpu.roll(own, block, 1)
            far_turned = pltpu.roll(far, block, 1)
            want_left = jnp.where(slot_low, pairs[0, 0, 0], 1 - pairs[0, 1, 0])
            want_right = jnp.where(slot_low, lax.rem(pairs[0, 0, 1], 2), 1 - lax.rem(pairs[0, 1, 1], 2))
            want_far = jnp.where(slot_low, pairs[0, 0, 1], pairs[0, 1, 1]) >= 2
            left = jnp.where(want_left == 0, own, own_turned)
            right = jnp.where(
                want_right == 0, jnp.where(want_far, far, own), jnp.where(want_far, far_turned, own_turned)
            )
            left_other, right_other = swap(left), swap(right)
            crossed = jnp.where(
                is_re, left * right + left_other * right_other, left * right_other - left_other * right
            )
            crossed_other = swap(crossed)
            power = crossed * crossed + crossed_other * crossed_other
            if j == 0:
                shared = shared_of(step)
                rows = lax.broadcasted_iota(jnp.int32, (step, LANES), 0) + i * step
                single = shared & (lax.rem(rows, height // 2) == 0)
                crossed = jnp.where(single, left * right, crossed)
                power = jnp.where(single, crossed * crossed, power)
            q = (crossed / (jnp.sqrt(power) + FLOOR)).astype(BF16).astype(F32)
            other = swap(q)
            for_cos, for_sin = q, jnp.where(is_re, -other, other)
            if j == 0:
                weight = jnp.where(single, 1.0, 2.0)
                if bottom:
                    for_cos = jnp.where(shared, jnp.where(is_re, 0.0, weight * other), for_cos)
                    for_sin = jnp.where(shared, jnp.where(is_re, 0.0, -2.0 * q), for_sin)
                else:
                    for_cos = jnp.where(shared, jnp.where(is_re, weight * q, 0.0), for_cos)
                    for_sin = jnp.where(shared, jnp.where(is_re, -2.0 * other, 0.0), for_sin)

                @pl.when(lax.rem(i, steps // 2) == 0)
                def _():
                    qfix[1 if bottom else 0] = q[0:16]

            ops[0, 0, at] = for_cos.astype(BF16)
            ops[0, 1, at] = for_sin.astype(BF16)
            return 0

        split = 0 < j == chunks - 1
        done = 0
        if split:
            for part in range(parts):
                if part:
                    partner_copy(j, part).wait_recv()
                first, last = part * steps // parts, (part + 1) * steps // parts
                lax.fori_loop(first, last, cross, 0)
                if part == parts - 1:
                    break
                done = (part + 1) * height // parts

                def share(i, _, since=part * height // parts, until=done):
                    at = pl.ds(pl.multiple_of(i * step, step), step)
                    z = mm(cos[at, since:until], ops[0, 0, since:until])
                    z = z + mm(sin[at, since:until], ops[0, 1, since:until])
                    zsum[at] = z + zsum[at] if since else z
                    return 0

                lax.fori_loop(0, steps, share, 0)
        else:
            lax.fori_loop(0, steps // 2, cross, 0)
            lax.fori_loop(steps // 2, steps, functools.partial(cross, bottom=True), 0)
        if j == 0:
            rows = lax.broadcasted_iota(jnp.int32, (16, LANES), 0)
            mark = (rows == 0) & shared_of(16)
            is_re = is_re_of(16)
            ops[0, 0, 0:16] = jnp.where(mark & ~is_re, qfix[1], ops[0, 0, 0:16].astype(F32)).astype(BF16)
            ops[0, 0, middle : middle + 16] = jnp.where(
                mark & is_re, swap(qfix[0]), ops[0, 0, middle : middle + 16].astype(F32)
            ).astype(BF16)
        for k in order + [0]:
            at = pl.ds(pl.multiple_of(lax.rem(me + k, n) * band, band), band)
            if split:
                z = mm(cos[at, done:], ops[0, 0, done:]) + mm(sin[at, done:], ops[0, 1, done:]) + zsum[at]
            else:
                z = mm(cos[at], ops[0, 0]) + mm(sin[at], ops[0, 1])
            if k:
                zsend[j, at] = z.astype(BF16)
                back_copy(j, k).start()
            else:
                zrecv[j, me] = z.astype(BF16)
        if j == 0:
            loads[6].wait()
        else:
            gather(j - 1)
    gather(chunks - 1)

    for j in range(chunks):
        for k in range(1, n):
            forward_copy(j, k).wait_send()
            back_copy(j, k).wait_send()
        if j > 0:
            for part in range(parts):
                partner_copy(j, part).wait_send()
    for k in range(n):
        far_copy(k).wait_send()


def local(tiles, pairs, counts):
    n = lax.axis_size("rows")
    nb = lax.axis_size("blk")
    groups, band, width = tiles.shape
    slots = pairs.shape[1]
    height = band * n
    cw = LANES // (2 * groups)
    chunks = width // 2 // n // cw
    cos_h, sin_h = dft_tables(height)
    forward, inverse = row_tables(width, n, cw)
    hann_h = np.repeat(hann(height).reshape(n, band, 1), LANES, axis=2)
    vmem = pl.BlockSpec(memory_space=pltpu.VMEM)
    smem = pl.BlockSpec(memory_space=pltpu.SMEM)
    hbm = pl.BlockSpec(memory_space=pltpu.HBM)
    dma = pltpu.SemaphoreType.DMA
    return pl.pallas_call(
        functools.partial(kernel, n, nb, cw),
        out_shape=jax.ShapeDtypeStruct((slots, band, width), F32),
        in_specs=[smem, smem, hbm, hbm, vmem, hbm, hbm, hbm, hbm],
        out_specs=vmem,
        scratch_shapes=[
            pltpu.VMEM(tiles.shape, F32),
            pltpu.VMEM((band, LANES), F32),
            pltpu.VMEM(forward.shape, BF16),
            pltpu.VMEM((height, height), BF16),
            pltpu.VMEM((height, height), BF16),
            pltpu.VMEM(inverse.shape, BF16),
            pltpu.VMEM(tiles.shape, BF16),
            pltpu.VMEM((chunks, n, band, LANES), BF16),
            pltpu.VMEM((chunks, height, LANES), BF16),
            pltpu.VMEM((height, LANES), BF16),
            pltpu.VMEM((2, 2, height, LANES), BF16),
            pltpu.VMEM((chunks, height, LANES), BF16),
            pltpu.VMEM((chunks, height, LANES), BF16),
            pltpu.VMEM((2, 16, LANES), F32),
            pltpu.VMEM((height, LANES), F32),
            pltpu.VMEM((chunks, height, LANES), BF16),
            pltpu.VMEM((chunks, n, band, LANES), BF16),
            dma((7,)),
            dma((chunks, n - 1)),
            dma((chunks, n - 1)),
            dma((n,)),
            dma((n,)),
            dma((chunks, 4)),
            dma((chunks, 4)),
            dma((chunks, n - 1)),
            dma((chunks, n - 1)),
        ],
        compiler_params=pltpu.CompilerParams(
            collective_id=0, has_side_effects=True, vmem_limit_bytes=51 * 1024 * 1024
        ),
    )(
        pairs,
        counts,
        tiles,
        jnp.asarray(hann_h),
        jnp.asarray(hann(width))[None, :],
        jnp.asarray(forward),
        jnp.asarray(cos_h.astype(ml_dtypes.bfloat16)),
        jnp.asarray(sin_h.astype(ml_dtypes.bfloat16)),
        jnp.asarray(inverse),
    )


def solution(mesh):
    return jax.shard_map(
        local,
        mesh=mesh,
        in_specs=(
            P(("parts", "blk"), "rows", None),
            P(("parts", "blk"), None, None),
            P(("parts", "blk")),
        ),
        out_specs=P(("parts", "blk"), "rows", None),
        check_vma=False,
    )
```

```python
import functools
import math

import jax
import jax.numpy as jnp
import ml_dtypes
import numpy as np
from jax import lax
from jax.experimental import pallas as pl
from jax.experimental.pallas import tpu as pltpu
from jax.sharding import PartitionSpec as P

FLOOR = 0.05
LANES = 128
MESH = pl.DeviceIdType.MESH
BF16 = jnp.bfloat16
F32 = jnp.float32


def dft_tables(length):
    index = np.arange(length)
    angle = 2.0 * math.pi / length * (index[:, None] * index[None, :] % length)
    factor = 1.0 / math.sqrt(length)
    return (
        (np.cos(angle) * factor).astype(ml_dtypes.bfloat16).astype(np.float32),
        (np.sin(angle) * factor).astype(ml_dtypes.bfloat16).astype(np.float32),
    )


def hann(length):
    return (0.5 - 0.5 * np.cos(2.0 * math.pi / length * np.arange(length))).astype(np.float32)


def row_tables(width, n, width_chunk):
    cos_w, sin_w = dft_tables(width)
    half = width // 2
    real, imag = cos_w[:, :half].copy(), -sin_w[:, :half]
    imag[:, 0] = cos_w[:, half]
    forward = np.stack([real, imag], 1).reshape(width, 2, n, -1, width_chunk).transpose(3, 0, 2, 1, 4)
    inverse_real, inverse_imag = 2.0 * real, 2.0 * imag
    inverse_real[:, 0], inverse_imag[:, 0] = real[:, 0], imag[:, 0]
    inverse = np.stack([inverse_real, inverse_imag], 1).reshape(width, 2, n, -1, width_chunk).transpose(3, 2, 1, 4, 0)
    chunks = half // n // width_chunk
    return (
        forward.reshape(chunks, width, n * 2 * width_chunk).astype(ml_dtypes.bfloat16),
        inverse.reshape(chunks, n * 2 * width_chunk, width).astype(ml_dtypes.bfloat16),
    )


def mm(a, b):
    return jnp.dot(a, b, preferred_element_type=F32)


def kernel(
    n, nb, cw,
    pairs, counts, tiles_hbm, window_hbm, fwd_hbm, cos_hbm, sin_hbm, inv_hbm,
    out,
    tiles, window, fwd, cos, sin, inv, shaded, fsend, frecv, far, ops, spec, pspec, qfix, zsend, zrecv, want, want_far_side,
    load_sem, fs, fr, gs, gr, zs, zr, bs, br, rs, rr, ws, wr,
):
    me = lax.axis_index("rows")
    blk = lax.axis_index("blk")
    partner = lax.rem(blk + nb // 2, nb)
    groups, band, width = tiles.shape
    height = cos.shape[0]
    chunks = spec.shape[0]
    step = min(256, height // 4)
    steps = height // step
    block = LANES // 2
    middle = height // 2
    parts = zs.shape[1]
    trade = chunks == 4
    given, kept = chunks - 2, chunks - 1
    role = blk // (nb // 2)

    def chunk_at(place):
        if trade and place >= given:
            return chunks - 1 - role if place == given else chunks - 2 + role
        return place

    order = [n // 2] + [k for k in range(1, n) if k != n // 2]

    loads = [
        pltpu.make_async_copy(src, dst, load_sem.at[i])
        for i, (src, dst) in enumerate(
            [
                (tiles_hbm, tiles),
                (window_hbm.at[me], window),
                (fwd_hbm.at[0], fwd.at[0]),
                (fwd_hbm.at[pl.ds(1, chunks - 1)], fwd.at[pl.ds(1, chunks - 1)]),
                (cos_hbm, cos),
                (sin_hbm, sin),
                (inv_hbm, inv),
            ]
        )
    ]
    for load in loads[:3]:
        load.start()

    barrier = pltpu.get_barrier_semaphore()
    for k in range(1, n):
        pl.semaphore_signal(barrier, inc=1, device_id={"rows": lax.rem(me + k, n)}, device_id_type=MESH)
    for k in range(n):
        pl.semaphore_signal(
            barrier, inc=1, device_id={"blk": partner, "rows": lax.rem(me + k, n)}, device_id_type=MESH
        )

    def lanes_of(rows):
        return lax.broadcasted_iota(jnp.int32, (rows, LANES), 1)

    def is_re_of(rows):
        return lax.rem(lanes_of(rows), 2 * cw) < cw

    def shared_of(rows):
        return lax.rem(lanes_of(rows), cw) == jnp.where(me == 0, 0, -1)

    def swap(x):
        return jnp.where(is_re_of(x.shape[0]), pltpu.roll(x, LANES - cw, 1), pltpu.roll(x, cw, 1))

    def forward_copy(j, k):
        return pltpu.make_async_remote_copy(
            src_ref=fsend.at[j, lax.rem(me + k, n)],
            dst_ref=frecv.at[j, pl.ds(pl.multiple_of(me * band, band), band)],
            send_sem=fs.at[j, k - 1],
            recv_sem=fr.at[j, k - 1],
            device_id={"rows": lax.rem(me + k, n)},
            device_id_type=MESH,
        )

    def far_copy(k):
        return pltpu.make_async_remote_copy(
            src_ref=fsend.at[0, lax.rem(me + k, n)],
            dst_ref=far.at[pl.ds(pl.multiple_of(me * band, band), band)],
            send_sem=gs.at[k],
            recv_sem=gr.at[k],
            device_id={"blk": partner, "rows": lax.rem(me + k, n)},
            device_id_type=MESH,
        )

    def want_copy():
        return pltpu.make_async_remote_copy(
            src_ref=want,
            dst_ref=want_far_side,
            send_sem=ws.at[0],
            recv_sem=wr.at[0],
            device_id={"blk": partner},
            device_id_type=MESH,
        )

    def result_copy(k):
        return pltpu.make_async_remote_copy(
            src_ref=zsend.at[given, pl.ds(pl.multiple_of(lax.rem(me + k, n) * band, band), band)],
            dst_ref=zrecv.at[given, me],
            send_sem=rs.at[k],
            recv_sem=rr.at[k],
            device_id={"blk": partner, "rows": lax.rem(me + k, n)},
            device_id_type=MESH,
        )

    def partner_copy(j, part):
        at = pl.ds(part * (height // parts), height // parts)
        return pltpu.make_async_remote_copy(
            src_ref=spec.at[j, at],
            dst_ref=pspec.at[kept if trade and j == given else j, at],
            send_sem=zs.at[j, part],
            recv_sem=zr.at[j, part],
            device_id={"blk": partner},
            device_id_type=MESH,
        )

    def back_copy(j, k):
        return pltpu.make_async_remote_copy(
            src_ref=zsend.at[j, pl.ds(pl.multiple_of(lax.rem(me + k, n) * band, band), band)],
            dst_ref=zrecv.at[j, me],
            send_sem=bs.at[j, k - 1],
            recv_sem=br.at[j, k - 1],
            device_id={"rows": lax.rem(me + k, n)},
            device_id_type=MESH,
        )

    loads[0].wait()
    loads[1].wait()
    for g in range(groups):
        shaded[g] = (tiles[g] * window[...]).astype(BF16)
    loads[2].wait()
    for load in loads[3:6]:
        load.start()
    low = lanes_of(band) < block

    def rows_to_columns(j):
        first = mm(shaded[0], fwd[chunk_at(j)])
        second = mm(shaded[1], fwd[chunk_at(j)])
        for m in range(n // 2):
            a = first[:, m * LANES : (m + 1) * LANES]
            b = second[:, m * LANES : (m + 1) * LANES]
            fsend[j, 2 * m] = jnp.where(low, a, pltpu.roll(b, block, 1)).astype(BF16)
            fsend[j, 2 * m + 1] = jnp.where(low, pltpu.roll(a, block, 1), b).astype(BF16)
        frecv[j, pl.ds(pl.multiple_of(me * band, band), band)] = fsend[j, me]

    def transform(source, target, shares):
        for half in range(2 if shares else 1):

            def operands(i, _, half=half):
                at = pl.ds(pl.multiple_of(i * step, step), step)
                y = source[at].astype(F32)
                is_re = is_re_of(step)
                if shares:
                    y = jnp.where(shared_of(step), jnp.where(is_re, swap(y) if half else y, 0.0), y)
                other = swap(y)
                ops[half, 0, at] = y.astype(BF16)
                ops[half, 1, at] = jnp.where(is_re, other, -other).astype(BF16)
                return 0

            lax.fori_loop(0, steps, operands, 0)
        for half in range(2):
            use = half if shares else 0

            def columns(i, _, use=use):
                at = pl.ds(pl.multiple_of(i * step, step), step)
                target[at] = (mm(cos[at], ops[use, 0]) + mm(sin[at], ops[use, 1])).astype(BF16)
                return 0

            lax.fori_loop(half * steps // 2, (half + 1) * steps // 2, columns, 0)
        if shares:
            rows = lax.broadcasted_iota(jnp.int32, (16, LANES), 0)
            mark = (rows == 0) & shared_of(16) & ~is_re_of(16)
            top = swap(mm(cos[middle : middle + 16], ops[0, 0]))
            bottom = swap(mm(cos[0:16], ops[1, 0]))
            target[0:16] = jnp.where(mark, top, target[0:16].astype(F32)).astype(BF16)
            target[middle : middle + 16] = jnp.where(
                mark, bottom, target[middle : middle + 16].astype(F32)
            ).astype(BF16)

    rows_to_columns(0)
    pl.semaphore_wait(barrier, 2 * n - 1)
    for k in range(n):
        far_copy(k).start()
    if trade:
        lanes = lanes_of(8)
        rows = lax.broadcasted_iota(jnp.int32, (8, LANES), 0)
        slot_low = lanes < block
        left_at = jnp.where(slot_low, pairs[0, 0, 0], 1 - pairs[0, 1, 0])
        right_at = jnp.where(slot_low, lax.rem(pairs[0, 0, 1], 2), 1 - lax.rem(pairs[0, 1, 1], 2))
        other_side = jnp.where(jnp.where(slot_low, pairs[0, 0, 1], pairs[0, 1, 1]) >= 2, 1, 0)
        picked = jnp.where(rows == 0, left_at, jnp.where(rows == 1, right_at, other_side))
        want[...] = picked.astype(F32)
        want_copy().start()
    loads[3].wait()
    middles = [1] if trade else list(range(1, chunks))
    turns = [given, 1, kept, 0] if trade else middles[:1] + [0] + middles[1:]
    rows_to_columns(turns[0])
    for k in order:
        forward_copy(turns[0], k).start()
    for at, j in enumerate(turns):
        later = turns[at + 1] if at + 1 < chunks else None
        if later:
            rows_to_columns(later)
        for k in range(1, n):
            forward_copy(j, k).wait_recv()
        if later is not None:
            for k in order:
                forward_copy(later, k).start()
        if at == 0:
            loads[4].wait()
            loads[5].wait()
            loads[6].start()
        transform(frecv.at[j], spec.at[j], j == 0)
        if j == given if trade else j > 0:
            for part in range(parts):
                partner_copy(j, part).start()

    def gather(j, first, last):
        for k in range(1, n):
            back_copy(j, k).wait_recv()
        add_up(j, first, last)

    def add_up(j, first, last):
        slabs = [[], []]
        for m in range(n // 2):
            a = zrecv[j, 2 * m].astype(F32)
            b = zrecv[j, 2 * m + 1].astype(F32)
            slabs[0].append(jnp.where(low, a, pltpu.roll(b, block, 1)).astype(BF16))
            slabs[1].append(jnp.where(low, pltpu.roll(a, block, 1), b).astype(BF16))
        for p in range(2):
            z = jnp.concatenate(slabs[p], axis=1)
            scale = jnp.where(p < counts[0], 1.0, 0.0).astype(F32)
            for c in range(0, width, 256):
                value = mm(z, inv[chunk_at(j), :, c : c + 256])
                if not first:
                    value = out[p, :, c : c + 256] + value
                if last:
                    value = value * scale
                out[p, :, c : c + 256] = value

    def whiten(own_ref, far_ref, picks, shares):
        def cross(i, _, bottom=False):
            at = pl.ds(pl.multiple_of(i * step, step), step)
            is_re = is_re_of(step)
            own = own_ref[at].astype(F32)
            far = far_ref[at].astype(F32)
            own_turned = pltpu.roll(own, block, 1)
            far_turned = pltpu.roll(far, block, 1)
            if picks is None:
                slot_low = lanes_of(step) < block
                want_left = jnp.where(slot_low, pairs[0, 0, 0], 1 - pairs[0, 1, 0]) == 0
                want_right = jnp.where(slot_low, lax.rem(pairs[0, 0, 1], 2), 1 - lax.rem(pairs[0, 1, 1], 2)) == 0
                want_far = jnp.where(slot_low, pairs[0, 0, 1], pairs[0, 1, 1]) >= 2
            else:
                want_left = jnp.broadcast_to(picks[0:1], (step, LANES)) < 0.5
                want_right = jnp.broadcast_to(picks[1:2], (step, LANES)) < 0.5
                want_far = jnp.broadcast_to(picks[2:3], (step, LANES)) > 0.5
            left = jnp.where(want_left, own, own_turned)
            right = jnp.where(want_right, jnp.where(want_far, far, own), jnp.where(want_far, far_turned, own_turned))
            left_other, right_other = swap(left), swap(right)
            crossed = jnp.where(
                is_re, left * right + left_other * right_other, left * right_other - left_other * right
            )
            crossed_other = swap(crossed)
            power = crossed * crossed + crossed_other * crossed_other
            if shares:
                shared = shared_of(step)
                rows = lax.broadcasted_iota(jnp.int32, (step, LANES), 0) + i * step
                single = shared & (lax.rem(rows, height // 2) == 0)
                crossed = jnp.where(single, left * right, crossed)
                power = jnp.where(single, crossed * crossed, power)
            q = (crossed / (jnp.sqrt(power) + FLOOR)).astype(BF16).astype(F32)
            other = swap(q)
            for_cos, for_sin = q, jnp.where(is_re, -other, other)
            if shares:
                weight = jnp.where(single, 1.0, 2.0)
                if bottom:
                    for_cos = jnp.where(shared, jnp.where(is_re, 0.0, weight * other), for_cos)
                    for_sin = jnp.where(shared, jnp.where(is_re, 0.0, -2.0 * q), for_sin)
                else:
                    for_cos = jnp.where(shared, jnp.where(is_re, weight * q, 0.0), for_cos)
                    for_sin = jnp.where(shared, jnp.where(is_re, -2.0 * other, 0.0), for_sin)

                @pl.when(lax.rem(i, steps // 2) == 0)
                def _():
                    qfix[1 if bottom else 0] = q[0:16]

            ops[0, 0, at] = for_cos.astype(BF16)
            ops[0, 1, at] = for_sin.astype(BF16)
            return 0

        lax.fori_loop(0, steps // 2, cross, 0)
        lax.fori_loop(steps // 2, steps, functools.partial(cross, bottom=True), 0)
        if shares:
            rows = lax.broadcasted_iota(jnp.int32, (16, LANES), 0)
            mark = (rows == 0) & shared_of(16)
            is_re = is_re_of(16)
            ops[0, 0, 0:16] = jnp.where(mark & ~is_re, qfix[1], ops[0, 0, 0:16].astype(F32)).astype(BF16)
            ops[0, 0, middle : middle + 16] = jnp.where(
                mark & is_re, swap(qfix[0]), ops[0, 0, middle : middle + 16].astype(F32)
            ).astype(BF16)

    def band_of(k):
        at = pl.ds(pl.multiple_of(lax.rem(me + k, n) * band, band), band)
        return at, (mm(cos[at], ops[0, 0]) + mm(sin[at], ops[0, 1])).astype(BF16)

    def own_slots(j):
        whiten(spec.at[j], pspec.at[j], None, j == 0)
        for k in order + [0]:
            at, z = band_of(k)
            if k:
                zsend[j, at] = z
                back_copy(j, k).start()
            else:
                zrecv[j, me] = z

    for k in range(n):
        far_copy(k).wait_recv()
    transform(far, pspec.at[0], True)
    own_slots(0)
    loads[6].wait()
    if trade:
        partner_copy(1, 0).start()
        for part in range(parts):
            partner_copy(given, part).wait_recv()
        for part in range(1, parts):
            partner_copy(1, part).start()
        want_copy().wait_recv()
        whiten(pspec.at[kept], spec.at[kept], want_far_side, False)
        for k in range(n):
            at, z = band_of(k)
            zsend[given, at] = z
        own_slots(kept)
        gather(0, True, False)
        result_copy(0).start()
        for part in range(parts):
            partner_copy(1, part).wait_recv()
        for k in range(1, n):
            result_copy(k).start()
        own_slots(1)
        gather(kept, False, False)
        gather(1, False, False)
        for k in range(n):
            result_copy(k).wait_recv()
        add_up(given, False, True)
    else:
        for j in middles:
            for part in range(parts):
                partner_copy(j, part).wait_recv()
            own_slots(j)
            gather(j - 1, j == 1, False)
        gather(chunks - 1, False, True)

    for j in range(chunks):
        for k in range(1, n):
            forward_copy(j, k).wait_send()
            if not (trade and j == given):
                back_copy(j, k).wait_send()
        if 0 < j and not (trade and j == kept):
            for part in range(parts):
                partner_copy(j, part).wait_send()
    for k in range(n):
        far_copy(k).wait_send()
        if trade:
            result_copy(k).wait_send()
    if trade:
        want_copy().wait_send()


def local(tiles, pairs, counts):
    n = lax.axis_size("rows")
    nb = lax.axis_size("blk")
    groups, band, width = tiles.shape
    slots = pairs.shape[1]
    height = band * n
    cw = LANES // (2 * groups)
    chunks = width // 2 // n // cw
    cos_h, sin_h = dft_tables(height)
    forward, inverse = row_tables(width, n, cw)
    window = (hann(height)[:, None] * hann(width)[None, :]).reshape(n, band, width)
    vmem = pl.BlockSpec(memory_space=pltpu.VMEM)
    smem = pl.BlockSpec(memory_space=pltpu.SMEM)
    hbm = pl.BlockSpec(memory_space=pltpu.HBM)
    dma = pltpu.SemaphoreType.DMA
    return pl.pallas_call(
        functools.partial(kernel, n, nb, cw),
        out_shape=jax.ShapeDtypeStruct((slots, band, width), F32),
        in_specs=[smem, smem, hbm, hbm, hbm, hbm, hbm, hbm],
        out_specs=vmem,
        scratch_shapes=[
            pltpu.VMEM(tiles.shape, F32),
            pltpu.VMEM((band, width), F32),
            pltpu.VMEM(forward.shape, BF16),
            pltpu.VMEM((height, height), BF16),
            pltpu.VMEM((height, height), BF16),
            pltpu.VMEM(inverse.shape, BF16),
            pltpu.VMEM(tiles.shape, BF16),
            pltpu.VMEM((chunks, n, band, LANES), BF16),
            pltpu.VMEM((chunks, height, LANES), BF16),
            pltpu.VMEM((height, LANES), BF16),
            pltpu.VMEM((2, 2, height, LANES), BF16),
            pltpu.VMEM((chunks, height, LANES), BF16),
            pltpu.VMEM((chunks, height, LANES), BF16),
            pltpu.VMEM((2, 16, LANES), F32),
            pltpu.VMEM((chunks, height, LANES), BF16),
            pltpu.VMEM((chunks, n, band, LANES), BF16),
            pltpu.VMEM((8, LANES), F32),
            pltpu.VMEM((8, LANES), F32),
            dma((7,)),
            dma((chunks, n - 1)),
            dma((chunks, n - 1)),
            dma((n,)),
            dma((n,)),
            dma((chunks, 4)),
            dma((chunks, 4)),
            dma((chunks, n - 1)),
            dma((chunks, n - 1)),
            dma((n,)),
            dma((n,)),
            dma((1,)),
            dma((1,)),
        ],
        compiler_params=pltpu.CompilerParams(
            collective_id=0, has_side_effects=True, vmem_limit_bytes=51 * 1024 * 1024
        ),
    )(
        pairs,
        counts,
        tiles,
        jnp.asarray(window),
        jnp.asarray(forward),
        jnp.asarray(cos_h.astype(ml_dtypes.bfloat16)),
        jnp.asarray(sin_h.astype(ml_dtypes.bfloat16)),
        jnp.asarray(inverse),
    )


def solution(mesh):
    return jax.shard_map(
        local,
        mesh=mesh,
        in_specs=(
            P(("parts", "blk"), "rows", None),
            P(("parts", "blk"), None, None),
            P(("parts", "blk")),
        ),
        out_specs=P(("parts", "blk"), "rows", None),
        check_vma=False,
    )
```

```python
import functools
import math

import jax
import jax.numpy as jnp
import ml_dtypes
import numpy as np
from jax import lax
from jax.experimental import pallas as pl
from jax.experimental.pallas import tpu as pltpu
from jax.sharding import PartitionSpec as P

FLOOR = 0.05
LANES = 128
MESH = pl.DeviceIdType.MESH
BF16 = jnp.bfloat16
F32 = jnp.float32


def dft_tables(length):
    index = np.arange(length)
    angle = 2.0 * math.pi / length * (index[:, None] * index[None, :] % length)
    factor = 1.0 / math.sqrt(length)
    return (
        (np.cos(angle) * factor).astype(ml_dtypes.bfloat16).astype(np.float32),
        (np.sin(angle) * factor).astype(ml_dtypes.bfloat16).astype(np.float32),
    )


def hann(length):
    return (0.5 - 0.5 * np.cos(2.0 * math.pi / length * np.arange(length))).astype(np.float32)


def row_tables(width, n, width_chunk):
    cos_w, sin_w = dft_tables(width)
    half = width // 2
    real, imag = cos_w[:, :half].copy(), -sin_w[:, :half]
    imag[:, 0] = cos_w[:, half]
    forward = np.stack([real, imag], 1).reshape(width, 2, n, -1, width_chunk).transpose(3, 0, 2, 1, 4)
    inverse_real, inverse_imag = 2.0 * real, 2.0 * imag
    inverse_real[:, 0], inverse_imag[:, 0] = real[:, 0], imag[:, 0]
    inverse = np.stack([inverse_real, inverse_imag], 1).reshape(width, 2, n, -1, width_chunk).transpose(3, 2, 1, 4, 0)
    chunks = half // n // width_chunk
    return (
        forward.reshape(chunks, width, n * 2 * width_chunk).astype(ml_dtypes.bfloat16),
        inverse.reshape(chunks, n * 2 * width_chunk, width).astype(ml_dtypes.bfloat16),
    )


def mm(a, b):
    return jnp.dot(a, b, preferred_element_type=F32)


def kernel(
    n, nb, cw,
    pairs, counts, tiles_hbm, window_hbm, fwd_hbm, cos_hbm, sin_hbm, inv_hbm,
    out,
    tiles, window, fwd, cos, sin, inv, shaded, fsend, frecv, far, ops, spec, pspec, qfix, zsend, zrecv, want, want_far_side,
    load_sem, fs, fr, gs, gr, zs, zr, bs, br, rs, rr, ws, wr,
):
    me = lax.axis_index("rows")
    blk = lax.axis_index("blk")
    partner = lax.rem(blk + nb // 2, nb)
    groups, band, width = tiles.shape
    height = cos.shape[0]
    chunks = spec.shape[0]
    step = min(256, height // 4)
    steps = height // step
    block = LANES // 2
    middle = height // 2
    parts = zs.shape[1]
    trade = chunks == 4
    given, kept = chunks - 2, chunks - 1
    role = blk // (nb // 2)

    def chunk_at(place):
        if trade and place >= given:
            return chunks - 1 - role if place == given else chunks - 2 + role
        return place

    order = [n // 2] + [k for k in range(1, n) if k != n // 2]

    loads = [
        pltpu.make_async_copy(src, dst, load_sem.at[i])
        for i, (src, dst) in enumerate(
            [
                (tiles_hbm, tiles),
                (window_hbm.at[me], window),
                (fwd_hbm, fwd),
                (cos_hbm, cos),
                (sin_hbm, sin),
                (inv_hbm, inv),
            ]
        )
    ]
    for load in loads[:3]:
        load.start()

    barrier = pltpu.get_barrier_semaphore()
    for k in range(1, n):
        pl.semaphore_signal(barrier, inc=1, device_id={"rows": lax.rem(me + k, n)}, device_id_type=MESH)
    for k in range(n):
        pl.semaphore_signal(
            barrier, inc=1, device_id={"blk": partner, "rows": lax.rem(me + k, n)}, device_id_type=MESH
        )

    def lanes_of(rows):
        return lax.broadcasted_iota(jnp.int32, (rows, LANES), 1)

    def is_re_of(rows):
        return lax.rem(lanes_of(rows), 2 * cw) < cw

    def shared_of(rows):
        return lax.rem(lanes_of(rows), cw) == jnp.where(me == 0, 0, -1)

    def swap(x):
        return jnp.where(is_re_of(x.shape[0]), pltpu.roll(x, LANES - cw, 1), pltpu.roll(x, cw, 1))

    def forward_copy(j, k):
        return pltpu.make_async_remote_copy(
            src_ref=fsend.at[j, lax.rem(me + k, n)],
            dst_ref=frecv.at[j, pl.ds(pl.multiple_of(me * band, band), band)],
            send_sem=fs.at[j, k - 1],
            recv_sem=fr.at[j, k - 1],
            device_id={"rows": lax.rem(me + k, n)},
            device_id_type=MESH,
        )

    def far_copy(k):
        return pltpu.make_async_remote_copy(
            src_ref=fsend.at[0, lax.rem(me + k, n)],
            dst_ref=far.at[pl.ds(pl.multiple_of(me * band, band), band)],
            send_sem=gs.at[k],
            recv_sem=gr.at[k],
            device_id={"blk": partner, "rows": lax.rem(me + k, n)},
            device_id_type=MESH,
        )

    def want_copy():
        return pltpu.make_async_remote_copy(
            src_ref=want,
            dst_ref=want_far_side,
            send_sem=ws.at[0],
            recv_sem=wr.at[0],
            device_id={"blk": partner},
            device_id_type=MESH,
        )

    def result_copy(k):
        return pltpu.make_async_remote_copy(
            src_ref=zsend.at[given, pl.ds(pl.multiple_of(lax.rem(me + k, n) * band, band), band)],
            dst_ref=zrecv.at[given, me],
            send_sem=rs.at[k],
            recv_sem=rr.at[k],
            device_id={"blk": partner, "rows": lax.rem(me + k, n)},
            device_id_type=MESH,
        )

    def partner_copy(j, part):
        at = pl.ds(part * (height // parts), height // parts)
        return pltpu.make_async_remote_copy(
            src_ref=spec.at[j, at],
            dst_ref=pspec.at[kept if trade and j == given else j, at],
            send_sem=zs.at[j, part],
            recv_sem=zr.at[j, part],
            device_id={"blk": partner},
            device_id_type=MESH,
        )

    def back_copy(j, k):
        return pltpu.make_async_remote_copy(
            src_ref=zsend.at[j, pl.ds(pl.multiple_of(lax.rem(me + k, n) * band, band), band)],
            dst_ref=zrecv.at[j, me],
            send_sem=bs.at[j, k - 1],
            recv_sem=br.at[j, k - 1],
            device_id={"rows": lax.rem(me + k, n)},
            device_id_type=MESH,
        )

    loads[0].wait()
    loads[1].wait()
    for g in range(groups):
        shaded[g] = (tiles[g] * window[...]).astype(BF16)
    loads[2].wait()
    for load in loads[3:]:
        load.start()
    low = lanes_of(band) < block

    def rows_to_columns(j):
        first = mm(shaded[0], fwd[chunk_at(j)])
        second = mm(shaded[1], fwd[chunk_at(j)])
        for m in range(n // 2):
            a = first[:, m * LANES : (m + 1) * LANES]
            b = second[:, m * LANES : (m + 1) * LANES]
            fsend[j, 2 * m] = jnp.where(low, a, pltpu.roll(b, block, 1)).astype(BF16)
            fsend[j, 2 * m + 1] = jnp.where(low, pltpu.roll(a, block, 1), b).astype(BF16)
        frecv[j, pl.ds(pl.multiple_of(me * band, band), band)] = fsend[j, me]

    def transform(source, target, shares):
        for half in range(2 if shares else 1):

            def operands(i, _, half=half):
                at = pl.ds(pl.multiple_of(i * step, step), step)
                y = source[at].astype(F32)
                is_re = is_re_of(step)
                if shares:
                    y = jnp.where(shared_of(step), jnp.where(is_re, swap(y) if half else y, 0.0), y)
                other = swap(y)
                ops[half, 0, at] = y.astype(BF16)
                ops[half, 1, at] = jnp.where(is_re, other, -other).astype(BF16)
                return 0

            lax.fori_loop(0, steps, operands, 0)
        for half in range(2):
            use = half if shares else 0

            def columns(i, _, use=use):
                at = pl.ds(pl.multiple_of(i * step, step), step)
                target[at] = (mm(cos[at], ops[use, 0]) + mm(sin[at], ops[use, 1])).astype(BF16)
                return 0

            lax.fori_loop(half * steps // 2, (half + 1) * steps // 2, columns, 0)
        if shares:
            rows = lax.broadcasted_iota(jnp.int32, (16, LANES), 0)
            mark = (rows == 0) & shared_of(16) & ~is_re_of(16)
            top = swap(mm(cos[middle : middle + 16], ops[0, 0]))
            bottom = swap(mm(cos[0:16], ops[1, 0]))
            target[0:16] = jnp.where(mark, top, target[0:16].astype(F32)).astype(BF16)
            target[middle : middle + 16] = jnp.where(
                mark, bottom, target[middle : middle + 16].astype(F32)
            ).astype(BF16)

    middles = [1] if trade else list(range(1, chunks))
    turns = [given, 1, kept, 0] if trade else middles[:1] + [0] + middles[1:]
    rows_to_columns(turns[0])
    pl.semaphore_wait(barrier, 2 * n - 1)
    for k in order:
        forward_copy(turns[0], k).start()
    rows_to_columns(0)
    for k in range(n):
        far_copy(k).start()
    if trade:
        lanes = lanes_of(8)
        rows = lax.broadcasted_iota(jnp.int32, (8, LANES), 0)
        slot_low = lanes < block
        left_at = jnp.where(slot_low, pairs[0, 0, 0], 1 - pairs[0, 1, 0])
        right_at = jnp.where(slot_low, lax.rem(pairs[0, 0, 1], 2), 1 - lax.rem(pairs[0, 1, 1], 2))
        other_side = jnp.where(jnp.where(slot_low, pairs[0, 0, 1], pairs[0, 1, 1]) >= 2, 1, 0)
        picked = jnp.where(rows == 0, left_at, jnp.where(rows == 1, right_at, other_side))
        want[...] = picked.astype(F32)
        want_copy().start()
    for at, j in enumerate(turns):
        later = turns[at + 1] if at + 1 < chunks else None
        if later:
            rows_to_columns(later)
        for k in range(1, n):
            forward_copy(j, k).wait_recv()
        if later is not None:
            for k in order:
                forward_copy(later, k).start()
        if at == 0:
            loads[3].wait()
            loads[4].wait()
        transform(frecv.at[j], spec.at[j], j == 0)
        if j == given if trade else j > 0:
            for part in range(parts):
                partner_copy(j, part).start()

    def gather(j, first, last):
        for k in range(1, n):
            back_copy(j, k).wait_recv()
        add_up(j, first, last)

    def add_up(j, first, last):
        slabs = [[], []]
        for m in range(n // 2):
            a = zrecv[j, 2 * m].astype(F32)
            b = zrecv[j, 2 * m + 1].astype(F32)
            slabs[0].append(jnp.where(low, a, pltpu.roll(b, block, 1)).astype(BF16))
            slabs[1].append(jnp.where(low, pltpu.roll(a, block, 1), b).astype(BF16))
        for p in range(2):
            z = jnp.concatenate(slabs[p], axis=1)
            scale = jnp.where(p < counts[0], 1.0, 0.0).astype(F32)
            for c in range(0, width, 256):
                value = mm(z, inv[chunk_at(j), :, c : c + 256])
                if not first:
                    value = out[p, :, c : c + 256] + value
                if last:
                    value = value * scale
                out[p, :, c : c + 256] = value

    def whiten(own_ref, far_ref, picks, shares):
        def cross(i, _, bottom=False):
            at = pl.ds(pl.multiple_of(i * step, step), step)
            is_re = is_re_of(step)
            own = own_ref[at].astype(F32)
            far = far_ref[at].astype(F32)
            own_turned = pltpu.roll(own, block, 1)
            far_turned = pltpu.roll(far, block, 1)
            if picks is None:
                slot_low = lanes_of(step) < block
                want_left = jnp.where(slot_low, pairs[0, 0, 0], 1 - pairs[0, 1, 0]) == 0
                want_right = jnp.where(slot_low, lax.rem(pairs[0, 0, 1], 2), 1 - lax.rem(pairs[0, 1, 1], 2)) == 0
                want_far = jnp.where(slot_low, pairs[0, 0, 1], pairs[0, 1, 1]) >= 2
            else:
                want_left = jnp.broadcast_to(picks[0:1], (step, LANES)) < 0.5
                want_right = jnp.broadcast_to(picks[1:2], (step, LANES)) < 0.5
                want_far = jnp.broadcast_to(picks[2:3], (step, LANES)) > 0.5
            left = jnp.where(want_left, own, own_turned)
            right = jnp.where(want_right, jnp.where(want_far, far, own), jnp.where(want_far, far_turned, own_turned))
            left_other, right_other = swap(left), swap(right)
            crossed = jnp.where(
                is_re, left * right + left_other * right_other, left * right_other - left_other * right
            )
            crossed_other = swap(crossed)
            power = crossed * crossed + crossed_other * crossed_other
            if shares:
                shared = shared_of(step)
                rows = lax.broadcasted_iota(jnp.int32, (step, LANES), 0) + i * step
                single = shared & (lax.rem(rows, height // 2) == 0)
                crossed = jnp.where(single, left * right, crossed)
                power = jnp.where(single, crossed * crossed, power)
            q = (crossed / (jnp.sqrt(power) + FLOOR)).astype(BF16).astype(F32)
            other = swap(q)
            for_cos, for_sin = q, jnp.where(is_re, -other, other)
            if shares:
                weight = jnp.where(single, 1.0, 2.0)
                if bottom:
                    for_cos = jnp.where(shared, jnp.where(is_re, 0.0, weight * other), for_cos)
                    for_sin = jnp.where(shared, jnp.where(is_re, 0.0, -2.0 * q), for_sin)
                else:
                    for_cos = jnp.where(shared, jnp.where(is_re, weight * q, 0.0), for_cos)
                    for_sin = jnp.where(shared, jnp.where(is_re, -2.0 * other, 0.0), for_sin)

                @pl.when(lax.rem(i, steps // 2) == 0)
                def _():
                    qfix[1 if bottom else 0] = q[0:16]

            ops[0, 0, at] = for_cos.astype(BF16)
            ops[0, 1, at] = for_sin.astype(BF16)
            return 0

        lax.fori_loop(0, steps // 2, cross, 0)
        lax.fori_loop(steps // 2, steps, functools.partial(cross, bottom=True), 0)
        if shares:
            rows = lax.broadcasted_iota(jnp.int32, (16, LANES), 0)
            mark = (rows == 0) & shared_of(16)
            is_re = is_re_of(16)
            ops[0, 0, 0:16] = jnp.where(mark & ~is_re, qfix[1], ops[0, 0, 0:16].astype(F32)).astype(BF16)
            ops[0, 0, middle : middle + 16] = jnp.where(
                mark & is_re, swap(qfix[0]), ops[0, 0, middle : middle + 16].astype(F32)
            ).astype(BF16)

    def band_of(k):
        at = pl.ds(pl.multiple_of(lax.rem(me + k, n) * band, band), band)
        return at, (mm(cos[at], ops[0, 0]) + mm(sin[at], ops[0, 1])).astype(BF16)

    def own_slots(j):
        whiten(spec.at[j], pspec.at[j], None, j == 0)
        for k in order + [0]:
            at, z = band_of(k)
            if k:
                zsend[j, at] = z
                back_copy(j, k).start()
            else:
                zrecv[j, me] = z

    for k in range(n):
        far_copy(k).wait_recv()
    transform(far, pspec.at[0], True)
    own_slots(0)
    loads[5].wait()
    if trade:
        for part in range(parts):
            partner_copy(1, part).start()
        for part in range(parts):
            partner_copy(given, part).wait_recv()
        want_copy().wait_recv()
        whiten(pspec.at[kept], spec.at[kept], want_far_side, False)
        for k in range(n):
            at, z = band_of(k)
            zsend[given, at] = z
        for k in range(n // 2):
            result_copy(k).start()
        own_slots(kept)
        gather(0, True, False)
        for part in range(parts):
            partner_copy(1, part).wait_recv()
        for k in range(n // 2, n):
            result_copy(k).start()
        own_slots(1)
        gather(kept, False, False)
        gather(1, False, False)
        for k in range(n):
            result_copy(k).wait_recv()
        add_up(given, False, True)
    else:
        for j in middles:
            for part in range(parts):
                partner_copy(j, part).wait_recv()
            own_slots(j)
            gather(j - 1, j == 1, False)
        gather(chunks - 1, False, True)

    for j in range(chunks):
        for k in range(1, n):
            forward_copy(j, k).wait_send()
            if not (trade and j == given):
                back_copy(j, k).wait_send()
        if 0 < j and not (trade and j == kept):
            for part in range(parts):
                partner_copy(j, part).wait_send()
    for k in range(n):
        far_copy(k).wait_send()
        if trade:
            result_copy(k).wait_send()
    if trade:
        want_copy().wait_send()


def local(tiles, pairs, counts):
    n = lax.axis_size("rows")
    nb = lax.axis_size("blk")
    groups, band, width = tiles.shape
    slots = pairs.shape[1]
    height = band * n
    cw = LANES // (2 * groups)
    chunks = width // 2 // n // cw
    cos_h, sin_h = dft_tables(height)
    forward, inverse = row_tables(width, n, cw)
    window = (hann(height)[:, None] * hann(width)[None, :]).reshape(n, band, width)
    vmem = pl.BlockSpec(memory_space=pltpu.VMEM)
    smem = pl.BlockSpec(memory_space=pltpu.SMEM)
    hbm = pl.BlockSpec(memory_space=pltpu.HBM)
    dma = pltpu.SemaphoreType.DMA
    return pl.pallas_call(
        functools.partial(kernel, n, nb, cw),
        out_shape=jax.ShapeDtypeStruct((slots, band, width), F32),
        in_specs=[smem, smem, hbm, hbm, hbm, hbm, hbm, hbm],
        out_specs=vmem,
        scratch_shapes=[
            pltpu.VMEM(tiles.shape, F32),
            pltpu.VMEM((band, width), F32),
            pltpu.VMEM(forward.shape, BF16),
            pltpu.VMEM((height, height), BF16),
            pltpu.VMEM((height, height), BF16),
            pltpu.VMEM(inverse.shape, BF16),
            pltpu.VMEM(tiles.shape, BF16),
            pltpu.VMEM((chunks, n, band, LANES), BF16),
            pltpu.VMEM((chunks, height, LANES), BF16),
            pltpu.VMEM((height, LANES), BF16),
            pltpu.VMEM((2, 2, height, LANES), BF16),
            pltpu.VMEM((chunks, height, LANES), BF16),
            pltpu.VMEM((chunks, height, LANES), BF16),
            pltpu.VMEM((2, 16, LANES), F32),
            pltpu.VMEM((chunks, height, LANES), BF16),
            pltpu.VMEM((chunks, n, band, LANES), BF16),
            pltpu.VMEM((8, LANES), F32),
            pltpu.VMEM((8, LANES), F32),
            dma((6,)),
            dma((chunks, n - 1)),
            dma((chunks, n - 1)),
            dma((n,)),
            dma((n,)),
            dma((chunks, 4)),
            dma((chunks, 4)),
            dma((chunks, n - 1)),
            dma((chunks, n - 1)),
            dma((n,)),
            dma((n,)),
            dma((1,)),
            dma((1,)),
        ],
        compiler_params=pltpu.CompilerParams(
            collective_id=0, has_side_effects=True, vmem_limit_bytes=51 * 1024 * 1024
        ),
    )(
        pairs,
        counts,
        tiles,
        jnp.asarray(window),
        jnp.asarray(forward),
        jnp.asarray(cos_h.astype(ml_dtypes.bfloat16)),
        jnp.asarray(sin_h.astype(ml_dtypes.bfloat16)),
        jnp.asarray(inverse),
    )


def solution(mesh):
    return jax.shard_map(
        local,
        mesh=mesh,
        in_specs=(
            P(("parts", "blk"), "rows", None),
            P(("parts", "blk"), None, None),
            P(("parts", "blk")),
        ),
        out_specs=P(("parts", "blk"), "rows", None),
        check_vma=False,
    )
```

```python
import functools
import math

import jax
import jax.numpy as jnp
import ml_dtypes
import numpy as np
from jax import lax
from jax.experimental import pallas as pl
from jax.experimental.pallas import tpu as pltpu
from jax.sharding import PartitionSpec as P

FLOOR = 0.05
LANES = 128
MESH = pl.DeviceIdType.MESH
BF16 = jnp.bfloat16
F32 = jnp.float32


def dft_tables(length):
    index = np.arange(length)
    angle = 2.0 * math.pi / length * (index[:, None] * index[None, :] % length)
    factor = 1.0 / math.sqrt(length)
    return (
        (np.cos(angle) * factor).astype(ml_dtypes.bfloat16).astype(np.float32),
        (np.sin(angle) * factor).astype(ml_dtypes.bfloat16).astype(np.float32),
    )


def hann(length):
    return (0.5 - 0.5 * np.cos(2.0 * math.pi / length * np.arange(length))).astype(np.float32)


def row_tables(width, n, width_chunk):
    cos_w, sin_w = dft_tables(width)
    half = width // 2
    real, imag = cos_w[:, :half].copy(), -sin_w[:, :half]
    imag[:, 0] = cos_w[:, half]
    forward = np.stack([real, imag], 1).reshape(width, 2, n, -1, width_chunk).transpose(3, 0, 2, 1, 4)
    inverse_real, inverse_imag = 2.0 * real, 2.0 * imag
    inverse_real[:, 0], inverse_imag[:, 0] = real[:, 0], imag[:, 0]
    inverse = np.stack([inverse_real, inverse_imag], 1).reshape(width, 2, n, -1, width_chunk).transpose(3, 2, 1, 4, 0)
    chunks = half // n // width_chunk
    return (
        forward.reshape(chunks, width, n * 2 * width_chunk).astype(ml_dtypes.bfloat16),
        inverse.reshape(chunks, n * 2 * width_chunk, width).astype(ml_dtypes.bfloat16),
    )


def mm(a, b):
    return jnp.dot(a, b, preferred_element_type=F32)


def kernel(
    n, nb, cw,
    pairs, counts, tiles_hbm, window_hbm, fwd_hbm, cos_hbm, sin_hbm, inv_hbm,
    out,
    tiles, window, fwd, cos, sin, inv, shaded, fsend, frecv, far, ops, spec, pspec, qfix, zsend, zrecv, want, want_far_side,
    load_sem, fs, fr, gs, gr, zs, zr, bs, br, rs, rr, ws, wr,
):
    me = lax.axis_index("rows")
    blk = lax.axis_index("blk")
    partner = lax.rem(blk + nb // 2, nb)
    groups, band, width = tiles.shape
    height = cos.shape[0]
    chunks = spec.shape[0]
    step = min(256, height // 4)
    steps = height // step
    block = LANES // 2
    middle = height // 2
    parts = zs.shape[1]
    trade = chunks == 4
    given, kept = chunks - 2, chunks - 1
    role = blk // (nb // 2)

    def chunk_at(place):
        if trade and place >= given:
            return chunks - 1 - role if place == given else chunks - 2 + role
        return place

    order = [n // 2] + [k for k in range(1, n) if k != n // 2]

    loads = [
        pltpu.make_async_copy(src, dst, load_sem.at[i])
        for i, (src, dst) in enumerate(
            [
                (tiles_hbm, tiles),
                (window_hbm.at[me], window),
                (fwd_hbm, fwd),
                (cos_hbm, cos),
                (sin_hbm, sin),
                (inv_hbm, inv),
            ]
        )
    ]
    for load in loads[:3]:
        load.start()

    barrier = pltpu.get_barrier_semaphore()
    for k in range(1, n):
        pl.semaphore_signal(barrier, inc=1, device_id={"rows": lax.rem(me + k, n)}, device_id_type=MESH)
    for k in range(n):
        pl.semaphore_signal(
            barrier, inc=1, device_id={"blk": partner, "rows": lax.rem(me + k, n)}, device_id_type=MESH
        )

    def lanes_of(rows):
        return lax.broadcasted_iota(jnp.int32, (rows, LANES), 1)

    def is_re_of(rows):
        return lax.rem(lanes_of(rows), 2 * cw) < cw

    def shared_of(rows):
        return lax.rem(lanes_of(rows), cw) == jnp.where(me == 0, 0, -1)

    def swap(x):
        return jnp.where(is_re_of(x.shape[0]), pltpu.roll(x, LANES - cw, 1), pltpu.roll(x, cw, 1))

    def forward_copy(j, k):
        return pltpu.make_async_remote_copy(
            src_ref=fsend.at[j, lax.rem(me + k, n)],
            dst_ref=frecv.at[j, pl.ds(pl.multiple_of(me * band, band), band)],
            send_sem=fs.at[j, k - 1],
            recv_sem=fr.at[j, k - 1],
            device_id={"rows": lax.rem(me + k, n)},
            device_id_type=MESH,
        )

    def far_copy(k):
        return pltpu.make_async_remote_copy(
            src_ref=fsend.at[0, lax.rem(me + k, n)],
            dst_ref=far.at[pl.ds(pl.multiple_of(me * band, band), band)],
            send_sem=gs.at[k],
            recv_sem=gr.at[k],
            device_id={"blk": partner, "rows": lax.rem(me + k, n)},
            device_id_type=MESH,
        )

    def want_copy():
        return pltpu.make_async_remote_copy(
            src_ref=want,
            dst_ref=want_far_side,
            send_sem=ws.at[0],
            recv_sem=wr.at[0],
            device_id={"blk": partner},
            device_id_type=MESH,
        )

    def result_copy(k):
        return pltpu.make_async_remote_copy(
            src_ref=zsend.at[given, pl.ds(pl.multiple_of(lax.rem(me + k, n) * band, band), band)],
            dst_ref=zrecv.at[given, me],
            send_sem=rs.at[k],
            recv_sem=rr.at[k],
            device_id={"blk": partner, "rows": lax.rem(me + k, n)},
            device_id_type=MESH,
        )

    def partner_copy(j, part):
        at = pl.ds(part * (height // parts), height // parts)
        return pltpu.make_async_remote_copy(
            src_ref=spec.at[j, at],
            dst_ref=pspec.at[kept if trade and j == given else j, at],
            send_sem=zs.at[j, part],
            recv_sem=zr.at[j, part],
            device_id={"blk": partner},
            device_id_type=MESH,
        )

    def back_copy(j, k):
        return pltpu.make_async_remote_copy(
            src_ref=zsend.at[j, pl.ds(pl.multiple_of(lax.rem(me + k, n) * band, band), band)],
            dst_ref=zrecv.at[j, me],
            send_sem=bs.at[j, k - 1],
            recv_sem=br.at[j, k - 1],
            device_id={"rows": lax.rem(me + k, n)},
            device_id_type=MESH,
        )

    loads[0].wait()
    loads[1].wait()
    for g in range(groups):
        shaded[g * band : (g + 1) * band] = (tiles[g] * window[...]).astype(BF16)
    loads[2].wait()
    for load in loads[3:]:
        load.start()
    low = lanes_of(band) < block

    def rows_to_columns(j):
        both = mm(shaded[...], fwd[chunk_at(j)])
        first, second = both[:band], both[band:]
        for m in range(n // 2):
            a = first[:, m * LANES : (m + 1) * LANES]
            b = second[:, m * LANES : (m + 1) * LANES]
            fsend[j, 2 * m] = jnp.where(low, a, pltpu.roll(b, block, 1)).astype(BF16)
            fsend[j, 2 * m + 1] = jnp.where(low, pltpu.roll(a, block, 1), b).astype(BF16)
        frecv[j, pl.ds(pl.multiple_of(me * band, band), band)] = fsend[j, me]

    def transform(source, target, shares):
        for half in range(2 if shares else 1):

            def operands(i, _, half=half):
                at = pl.ds(pl.multiple_of(i * step, step), step)
                y = source[at].astype(F32)
                is_re = is_re_of(step)
                if shares:
                    y = jnp.where(shared_of(step), jnp.where(is_re, swap(y) if half else y, 0.0), y)
                other = swap(y)
                ops[half, 0, at] = y.astype(BF16)
                ops[half, 1, at] = jnp.where(is_re, other, -other).astype(BF16)
                return 0

            lax.fori_loop(0, steps, operands, 0)
        for half in range(2 if shares else 1):
            first, last = (half * middle, (half + 1) * middle) if shares else (0, height)
            target[first:last] = (mm(cos[first:last], ops[half, 0]) + mm(sin[first:last], ops[half, 1])).astype(BF16)
        if shares:
            rows = lax.broadcasted_iota(jnp.int32, (16, LANES), 0)
            mark = (rows == 0) & shared_of(16) & ~is_re_of(16)
            top = swap(mm(cos[middle : middle + 16], ops[0, 0]))
            bottom = swap(mm(cos[0:16], ops[1, 0]))
            target[0:16] = jnp.where(mark, top, target[0:16].astype(F32)).astype(BF16)
            target[middle : middle + 16] = jnp.where(
                mark, bottom, target[middle : middle + 16].astype(F32)
            ).astype(BF16)

    middles = [1] if trade else list(range(1, chunks))
    turns = [given, 1, kept, 0] if trade else middles[:1] + [0] + middles[1:]
    rows_to_columns(turns[0])
    pl.semaphore_wait(barrier, 2 * n - 1)
    for k in order:
        forward_copy(turns[0], k).start()
    rows_to_columns(0)
    for k in range(n):
        far_copy(k).start()
    if trade:
        lanes = lanes_of(8)
        rows = lax.broadcasted_iota(jnp.int32, (8, LANES), 0)
        slot_low = lanes < block
        left_at = jnp.where(slot_low, pairs[0, 0, 0], 1 - pairs[0, 1, 0])
        right_at = jnp.where(slot_low, lax.rem(pairs[0, 0, 1], 2), 1 - lax.rem(pairs[0, 1, 1], 2))
        other_side = jnp.where(jnp.where(slot_low, pairs[0, 0, 1], pairs[0, 1, 1]) >= 2, 1, 0)
        picked = jnp.where(rows == 0, left_at, jnp.where(rows == 1, right_at, other_side))
        want[...] = picked.astype(F32)
        want_copy().start()
    for at, j in enumerate(turns):
        later = turns[at + 1] if at + 1 < chunks else None
        if later:
            rows_to_columns(later)
        for k in range(1, n):
            forward_copy(j, k).wait_recv()
        if later is not None:
            for k in order:
                forward_copy(later, k).start()
        if at == 0:
            loads[3].wait()
            loads[4].wait()
        transform(frecv.at[j], spec.at[j], j == 0)
        if j == given if trade else j > 0:
            for part in range(parts):
                partner_copy(j, part).start()

    def gather(j, first, last):
        for k in range(1, n):
            back_copy(j, k).wait_recv()
        add_up(j, first, last)

    def add_up(j, first, last):
        slabs = [[], []]
        for m in range(n // 2):
            a = zrecv[j, 2 * m].astype(F32)
            b = zrecv[j, 2 * m + 1].astype(F32)
            slabs[0].append(jnp.where(low, a, pltpu.roll(b, block, 1)).astype(BF16))
            slabs[1].append(jnp.where(low, pltpu.roll(a, block, 1), b).astype(BF16))
        z = jnp.concatenate([jnp.concatenate(slab, axis=1) for slab in slabs], axis=0)
        for c in range(0, width, 256):
            both = mm(z, inv[chunk_at(j), :, c : c + 256])
            for p in range(2):
                value = both[p * band : (p + 1) * band]
                if not first:
                    value = out[p, :, c : c + 256] + value
                if last:
                    value = value * jnp.where(p < counts[0], 1.0, 0.0).astype(F32)
                out[p, :, c : c + 256] = value

    def whiten(own_ref, far_ref, picks, shares):
        def cross(i, _, bottom=False):
            at = pl.ds(pl.multiple_of(i * step, step), step)
            is_re = is_re_of(step)
            own = own_ref[at].astype(F32)
            far = far_ref[at].astype(F32)
            own_turned = pltpu.roll(own, block, 1)
            far_turned = pltpu.roll(far, block, 1)
            if picks is None:
                slot_low = lanes_of(step) < block
                want_left = jnp.where(slot_low, pairs[0, 0, 0], 1 - pairs[0, 1, 0]) == 0
                want_right = jnp.where(slot_low, lax.rem(pairs[0, 0, 1], 2), 1 - lax.rem(pairs[0, 1, 1], 2)) == 0
                want_far = jnp.where(slot_low, pairs[0, 0, 1], pairs[0, 1, 1]) >= 2
            else:
                want_left = jnp.broadcast_to(picks[0:1], (step, LANES)) < 0.5
                want_right = jnp.broadcast_to(picks[1:2], (step, LANES)) < 0.5
                want_far = jnp.broadcast_to(picks[2:3], (step, LANES)) > 0.5
            left = jnp.where(want_left, own, own_turned)
            right = jnp.where(want_right, jnp.where(want_far, far, own), jnp.where(want_far, far_turned, own_turned))
            left_other, right_other = swap(left), swap(right)
            crossed = jnp.where(
                is_re, left * right + left_other * right_other, left * right_other - left_other * right
            )
            crossed_other = swap(crossed)
            power = crossed * crossed + crossed_other * crossed_other
            if shares:
                shared = shared_of(step)
                rows = lax.broadcasted_iota(jnp.int32, (step, LANES), 0) + i * step
                single = shared & (lax.rem(rows, height // 2) == 0)
                crossed = jnp.where(single, left * right, crossed)
                power = jnp.where(single, crossed * crossed, power)
            q = (crossed / (jnp.sqrt(power) + FLOOR)).astype(BF16).astype(F32)
            other = swap(q)
            for_cos, for_sin = q, jnp.where(is_re, -other, other)
            if shares:
                weight = jnp.where(single, 1.0, 2.0)
                if bottom:
                    for_cos = jnp.where(shared, jnp.where(is_re, 0.0, weight * other), for_cos)
                    for_sin = jnp.where(shared, jnp.where(is_re, 0.0, -2.0 * q), for_sin)
                else:
                    for_cos = jnp.where(shared, jnp.where(is_re, weight * q, 0.0), for_cos)
                    for_sin = jnp.where(shared, jnp.where(is_re, -2.0 * other, 0.0), for_sin)

                @pl.when(lax.rem(i, steps // 2) == 0)
                def _():
                    qfix[1 if bottom else 0] = q[0:16]

            ops[0, 0, at] = for_cos.astype(BF16)
            ops[0, 1, at] = for_sin.astype(BF16)
            return 0

        lax.fori_loop(0, steps // 2, cross, 0)
        lax.fori_loop(steps // 2, steps, functools.partial(cross, bottom=True), 0)
        if shares:
            rows = lax.broadcasted_iota(jnp.int32, (16, LANES), 0)
            mark = (rows == 0) & shared_of(16)
            is_re = is_re_of(16)
            ops[0, 0, 0:16] = jnp.where(mark & ~is_re, qfix[1], ops[0, 0, 0:16].astype(F32)).astype(BF16)
            ops[0, 0, middle : middle + 16] = jnp.where(
                mark & is_re, swap(qfix[0]), ops[0, 0, middle : middle + 16].astype(F32)
            ).astype(BF16)

    def invert(j):
        zsend[j] = (mm(cos[...], ops[0, 0]) + mm(sin[...], ops[0, 1])).astype(BF16)

    def own_slots(j):
        whiten(spec.at[j], pspec.at[j], None, j == 0)
        invert(j)
        for k in order:
            back_copy(j, k).start()
        zrecv[j, me] = zsend[j, pl.ds(pl.multiple_of(me * band, band), band)]

    for k in range(n):
        far_copy(k).wait_recv()
    transform(far, pspec.at[0], True)
    own_slots(0)
    loads[5].wait()
    if trade:
        for part in range(parts):
            partner_copy(1, part).start()
        for part in range(parts):
            partner_copy(given, part).wait_recv()
        want_copy().wait_recv()
        whiten(pspec.at[kept], spec.at[kept], want_far_side, False)
        invert(given)
        for k in range(n // 2):
            result_copy(k).start()
        own_slots(kept)
        gather(0, True, False)
        for part in range(parts):
            partner_copy(1, part).wait_recv()
        for k in range(n // 2, n):
            result_copy(k).start()
        own_slots(1)
        gather(kept, False, False)
        gather(1, False, False)
        for k in range(n):
            result_copy(k).wait_recv()
        add_up(given, False, True)
    else:
        for j in middles:
            for part in range(parts):
                partner_copy(j, part).wait_recv()
            own_slots(j)
            gather(j - 1, j == 1, False)
        gather(chunks - 1, False, True)

    for j in range(chunks):
        for k in range(1, n):
            forward_copy(j, k).wait_send()
            if not (trade and j == given):
                back_copy(j, k).wait_send()
        if 0 < j and not (trade and j == kept):
            for part in range(parts):
                partner_copy(j, part).wait_send()
    for k in range(n):
        far_copy(k).wait_send()
        if trade:
            result_copy(k).wait_send()
    if trade:
        want_copy().wait_send()


def local(tiles, pairs, counts):
    n = lax.axis_size("rows")
    nb = lax.axis_size("blk")
    groups, band, width = tiles.shape
    slots = pairs.shape[1]
    height = band * n
    cw = LANES // (2 * groups)
    chunks = width // 2 // n // cw
    cos_h, sin_h = dft_tables(height)
    forward, inverse = row_tables(width, n, cw)
    window = (hann(height)[:, None] * hann(width)[None, :]).reshape(n, band, width)
    vmem = pl.BlockSpec(memory_space=pltpu.VMEM)
    smem = pl.BlockSpec(memory_space=pltpu.SMEM)
    hbm = pl.BlockSpec(memory_space=pltpu.HBM)
    dma = pltpu.SemaphoreType.DMA
    return pl.pallas_call(
        functools.partial(kernel, n, nb, cw),
        out_shape=jax.ShapeDtypeStruct((slots, band, width), F32),
        in_specs=[smem, smem, hbm, hbm, hbm, hbm, hbm, hbm],
        out_specs=vmem,
        scratch_shapes=[
            pltpu.VMEM(tiles.shape, F32),
            pltpu.VMEM((band, width), F32),
            pltpu.VMEM(forward.shape, BF16),
            pltpu.VMEM((height, height), BF16),
            pltpu.VMEM((height, height), BF16),
            pltpu.VMEM(inverse.shape, BF16),
            pltpu.VMEM((groups * band, width), BF16),
            pltpu.VMEM((chunks, n, band, LANES), BF16),
            pltpu.VMEM((chunks, height, LANES), BF16),
            pltpu.VMEM((height, LANES), BF16),
            pltpu.VMEM((2, 2, height, LANES), BF16),
            pltpu.VMEM((chunks, height, LANES), BF16),
            pltpu.VMEM((chunks, height, LANES), BF16),
            pltpu.VMEM((2, 16, LANES), F32),
            pltpu.VMEM((chunks, height, LANES), BF16),
            pltpu.VMEM((chunks, n, band, LANES), BF16),
            pltpu.VMEM((8, LANES), F32),
            pltpu.VMEM((8, LANES), F32),
            dma((6,)),
            dma((chunks, n - 1)),
            dma((chunks, n - 1)),
            dma((n,)),
            dma((n,)),
            dma((chunks, 4)),
            dma((chunks, 4)),
            dma((chunks, n - 1)),
            dma((chunks, n - 1)),
            dma((n,)),
            dma((n,)),
            dma((1,)),
            dma((1,)),
        ],
        compiler_params=pltpu.CompilerParams(
            collective_id=0, has_side_effects=True, vmem_limit_bytes=51 * 1024 * 1024
        ),
    )(
        pairs,
        counts,
        tiles,
        jnp.asarray(window),
        jnp.asarray(forward),
        jnp.asarray(cos_h.astype(ml_dtypes.bfloat16)),
        jnp.asarray(sin_h.astype(ml_dtypes.bfloat16)),
        jnp.asarray(inverse),
    )


def solution(mesh):
    return jax.shard_map(
        local,
        mesh=mesh,
        in_specs=(
            P(("parts", "blk"), "rows", None),
            P(("parts", "blk"), None, None),
            P(("parts", "blk")),
        ),
        out_specs=P(("parts", "blk"), "rows", None),
        check_vma=False,
    )
```

```python
import functools
import math

import jax
import jax.numpy as jnp
import ml_dtypes
import numpy as np
from jax import lax
from jax.experimental import pallas as pl
from jax.experimental.pallas import tpu as pltpu
from jax.sharding import PartitionSpec as P

FLOOR = 0.05
LANES = 128
MESH = pl.DeviceIdType.MESH
BF16 = jnp.bfloat16
F32 = jnp.float32


def dft_tables(length):
    index = np.arange(length)
    angle = 2.0 * math.pi / length * (index[:, None] * index[None, :] % length)
    factor = 1.0 / math.sqrt(length)
    return (
        (np.cos(angle) * factor).astype(ml_dtypes.bfloat16).astype(np.float32),
        (np.sin(angle) * factor).astype(ml_dtypes.bfloat16).astype(np.float32),
    )


def hann(length):
    return (0.5 - 0.5 * np.cos(2.0 * math.pi / length * np.arange(length))).astype(np.float32)


def row_tables(width, n, width_chunk):
    cos_w, sin_w = dft_tables(width)
    half = width // 2
    real, imag = cos_w[:, :half].copy(), -sin_w[:, :half]
    imag[:, 0] = cos_w[:, half]
    forward = np.stack([real, imag], 1).reshape(width, 2, n, -1, width_chunk).transpose(3, 0, 2, 1, 4)
    inverse_real, inverse_imag = 2.0 * real, 2.0 * imag
    inverse_real[:, 0], inverse_imag[:, 0] = real[:, 0], imag[:, 0]
    inverse = np.stack([inverse_real, inverse_imag], 1).reshape(width, 2, n, -1, width_chunk).transpose(3, 2, 1, 4, 0)
    chunks = half // n // width_chunk
    return (
        forward.reshape(chunks, width, n * 2 * width_chunk).astype(ml_dtypes.bfloat16),
        inverse.reshape(chunks, n * 2 * width_chunk, width).astype(ml_dtypes.bfloat16),
    )


def mm(a, b):
    return jnp.dot(a, b, preferred_element_type=F32)


def kernel(
    n, nb, cw,
    pairs, counts, tiles_hbm, window_hbm, fwd_hbm, cos_hbm, sin_hbm, inv_hbm,
    out,
    tiles, window, fwd, cos, sin, inv, shaded, fsend, frecv, far, ops, spec, pspec, qfix, zsum, zsend, zrecv,
    load_sem, fs, fr, gs, gr, zs, zr, bs, br,
):
    me = lax.axis_index("rows")
    blk = lax.axis_index("blk")
    partner = lax.rem(blk + nb // 2, nb)
    groups, band, width = tiles.shape
    height = cos.shape[0]
    chunks = spec.shape[0]
    step = min(256, height // 2)
    steps = height // step
    block = LANES // 2
    middle = height // 2
    order = [n // 2] + [k for k in range(1, n) if k != n // 2]

    loads = [
        pltpu.make_async_copy(src, dst, load_sem.at[i])
        for i, (src, dst) in enumerate(
            [(tiles_hbm, tiles), (window_hbm.at[me], window), (fwd_hbm, fwd), (cos_hbm, cos), (sin_hbm, sin), (inv_hbm, inv)]
        )
    ]
    for load in loads[:3]:
        load.start()

    barrier = pltpu.get_barrier_semaphore()
    for k in range(1, n):
        pl.semaphore_signal(barrier, inc=1, device_id={"rows": lax.rem(me + k, n)}, device_id_type=MESH)
    for k in range(n):
        pl.semaphore_signal(
            barrier, inc=1, device_id={"blk": partner, "rows": lax.rem(me + k, n)}, device_id_type=MESH
        )

    def lanes_of(rows):
        return lax.broadcasted_iota(jnp.int32, (rows, LANES), 1)

    def is_re_of(rows):
        return lax.rem(lanes_of(rows), 2 * cw) < cw

    def shared_of(rows):
        return lax.rem(lanes_of(rows), cw) == jnp.where(me == 0, 0, -1)

    def swap(x):
        return jnp.where(is_re_of(x.shape[0]), pltpu.roll(x, LANES - cw, 1), pltpu.roll(x, cw, 1))

    def forward_copy(j, k):
        return pltpu.make_async_remote_copy(
            src_ref=fsend.at[j, lax.rem(me + k, n)],
            dst_ref=frecv.at[j, pl.ds(pl.multiple_of(me * band, band), band)],
            send_sem=fs.at[j, k - 1],
            recv_sem=fr.at[j, k - 1],
            device_id={"rows": lax.rem(me + k, n)},
            device_id_type=MESH,
        )

    def far_copy(k):
        return pltpu.make_async_remote_copy(
            src_ref=fsend.at[0, lax.rem(me + k, n)],
            dst_ref=far.at[pl.ds(pl.multiple_of(me * band, band), band)],
            send_sem=gs.at[k],
            recv_sem=gr.at[k],
            device_id={"blk": partner, "rows": lax.rem(me + k, n)},
            device_id_type=MESH,
        )

    def partner_copy(j, half):
        at = pl.ds(half * middle, middle)
        return pltpu.make_async_remote_copy(
            src_ref=spec.at[j, at],
            dst_ref=pspec.at[j, at],
            send_sem=zs.at[j, half],
            recv_sem=zr.at[j, half],
            device_id={"blk": partner},
            device_id_type=MESH,
        )

    def back_copy(j, k):
        return pltpu.make_async_remote_copy(
            src_ref=zsend.at[j, pl.ds(pl.multiple_of(lax.rem(me + k, n) * band, band), band)],
            dst_ref=zrecv.at[j, me],
            send_sem=bs.at[j, k - 1],
            recv_sem=br.at[j, k - 1],
            device_id={"rows": lax.rem(me + k, n)},
            device_id_type=MESH,
        )

    loads[0].wait()
    loads[1].wait()
    for g in range(groups):
        shaded[g] = (tiles[g] * window[...]).astype(BF16)
    loads[2].wait()
    for load in loads[3:]:
        load.start()
    low = lanes_of(band) < block

    def rows_to_columns(j):
        first = mm(shaded[0], fwd[j])
        second = mm(shaded[1], fwd[j])
        for m in range(n // 2):
            a = first[:, m * LANES : (m + 1) * LANES]
            b = second[:, m * LANES : (m + 1) * LANES]
            fsend[j, 2 * m] = jnp.where(low, a, pltpu.roll(b, block, 1)).astype(BF16)
            fsend[j, 2 * m + 1] = jnp.where(low, pltpu.roll(a, block, 1), b).astype(BF16)
        frecv[j, pl.ds(pl.multiple_of(me * band, band), band)] = fsend[j, me]

    def transform(source, target, shares):
        for half in range(2 if shares else 1):

            def operands(i, _, half=half):
                at = pl.ds(pl.multiple_of(i * step, step), step)
                y = source[at].astype(F32)
                is_re = is_re_of(step)
                if shares:
                    y = jnp.where(shared_of(step), jnp.where(is_re, swap(y) if half else y, 0.0), y)
                other = swap(y)
                ops[half, 0, at] = y.astype(BF16)
                ops[half, 1, at] = jnp.where(is_re, other, -other).astype(BF16)
                return 0

            lax.fori_loop(0, steps, operands, 0)
        for half in range(2):
            use = half if shares else 0

            def columns(i, _, use=use):
                at = pl.ds(pl.multiple_of(i * step, step), step)
                target[at] = (mm(cos[at], ops[use, 0]) + mm(sin[at], ops[use, 1])).astype(BF16)
                return 0

            lax.fori_loop(half * steps // 2, (half + 1) * steps // 2, columns, 0)
        if shares:
            rows = lax.broadcasted_iota(jnp.int32, (16, LANES), 0)
            mark = (rows == 0) & shared_of(16) & ~is_re_of(16)
            top = swap(mm(cos[middle : middle + 16], ops[0, 0]))
            bottom = swap(mm(cos[0:16], ops[1, 0]))
            target[0:16] = jnp.where(mark, top, target[0:16].astype(F32)).astype(BF16)
            target[middle : middle + 16] = jnp.where(
                mark, bottom, target[middle : middle + 16].astype(F32)
            ).astype(BF16)

    rows_to_columns(0)
    pl.semaphore_wait(barrier, 2 * n - 1)
    for k in order:
        forward_copy(0, k).start()
    for k in range(n):
        far_copy(k).start()
    for j in range(chunks):
        if j + 1 < chunks:
            rows_to_columns(j + 1)
        for k in range(1, n):
            forward_copy(j, k).wait_recv()
        if j + 1 < chunks:
            for k in order:
                forward_copy(j + 1, k).start()
        if j == 0:
            loads[3].wait()
            loads[4].wait()
        transform(frecv.at[j], spec.at[j], j == 0)
        if j == 1:
            for half in range(2):
                partner_copy(j, half).start()

    def gather(j):
        for k in range(1, n):
            back_copy(j, k).wait_recv()
        parts = [[], []]
        for m in range(n // 2):
            a = zrecv[j, 2 * m].astype(F32)
            b = zrecv[j, 2 * m + 1].astype(F32)
            parts[0].append(jnp.where(low, a, pltpu.roll(b, block, 1)).astype(BF16))
            parts[1].append(jnp.where(low, pltpu.roll(a, block, 1), b).astype(BF16))
        for p in range(2):
            z = jnp.concatenate(parts[p], axis=1)
            scale = jnp.where(p < counts[0], 1.0, 0.0).astype(F32)
            for c in range(0, width, 256):
                value = mm(z, inv[j, :, c : c + 256])
                if j > 0:
                    value = out[p, :, c : c + 256] + value
                if j == chunks - 1:
                    value = value * scale
                out[p, :, c : c + 256] = value

    for j in range(chunks):
        if j == 0:
            for k in range(n):
                far_copy(k).wait_recv()
        else:
            partner_copy(j, 0).wait_recv()
            if j < chunks - 1:
                partner_copy(j, 1).wait_recv()
        if j + 2 < chunks:
            for half in range(2):
                partner_copy(j + 2, half).start()
        if j == 0:
            transform(far, pspec.at[0], True)

        def cross(i, _, j=j, bottom=False):
            at = pl.ds(pl.multiple_of(i * step, step), step)
            is_re = is_re_of(step)
            slot_low = lanes_of(step) < block
            own = spec[j, at].astype(F32)
            far = pspec[j, at].astype(F32)
            own_turned = pltpu.roll(own, block, 1)
            far_turned = pltpu.roll(far, block, 1)
            want_left = jnp.where(slot_low, pairs[0, 0, 0], 1 - pairs[0, 1, 0])
            want_right = jnp.where(slot_low, lax.rem(pairs[0, 0, 1], 2), 1 - lax.rem(pairs[0, 1, 1], 2))
            want_far = jnp.where(slot_low, pairs[0, 0, 1], pairs[0, 1, 1]) >= 2
            left = jnp.where(want_left == 0, own, own_turned)
            right = jnp.where(
                want_right == 0, jnp.where(want_far, far, own), jnp.where(want_far, far_turned, own_turned)
            )
            left_other, right_other = swap(left), swap(right)
            crossed = jnp.where(
                is_re, left * right + left_other * right_other, left * right_other - left_other * right
            )
            crossed_other = swap(crossed)
            power = crossed * crossed + crossed_other * crossed_other
            if j == 0:
                shared = shared_of(step)
                rows = lax.broadcasted_iota(jnp.int32, (step, LANES), 0) + i * step
                single = shared & (lax.rem(rows, height // 2) == 0)
                crossed = jnp.where(single, left * right, crossed)
                power = jnp.where(single, crossed * crossed, power)
            q = (crossed / (jnp.sqrt(power) + FLOOR)).astype(BF16).astype(F32)
            other = swap(q)
            for_cos, for_sin = q, jnp.where(is_re, -other, other)
            if j == 0:
                weight = jnp.where(single, 1.0, 2.0)
                if bottom:
                    for_cos = jnp.where(shared, jnp.where(is_re, 0.0, weight * other), for_cos)
                    for_sin = jnp.where(shared, jnp.where(is_re, 0.0, -2.0 * q), for_sin)
                else:
                    for_cos = jnp.where(shared, jnp.where(is_re, weight * q, 0.0), for_cos)
                    for_sin = jnp.where(shared, jnp.where(is_re, -2.0 * other, 0.0), for_sin)

                @pl.when(lax.rem(i, steps // 2) == 0)
                def _():
                    qfix[1 if bottom else 0] = q[0:16]

            ops[0, 0, at] = for_cos.astype(BF16)
            ops[0, 1, at] = for_sin.astype(BF16)
            return 0

        lax.fori_loop(0, steps // 2, functools.partial(cross, bottom=False), 0)
        split = 0 < j == chunks - 1
        if split:

            def part(i, _):
                at = pl.ds(pl.multiple_of(i * step, step), step)
                zsum[at] = mm(cos[at, 0:middle], ops[0, 0, 0:middle]) + mm(sin[at, 0:middle], ops[0, 1, 0:middle])
                return 0

            lax.fori_loop(0, steps, part, 0)
            partner_copy(j, 1).wait_recv()
        lax.fori_loop(steps // 2, steps, functools.partial(cross, bottom=True), 0)
        if j == 0:
            rows = lax.broadcasted_iota(jnp.int32, (16, LANES), 0)
            mark = (rows == 0) & shared_of(16)
            is_re = is_re_of(16)
            ops[0, 0, 0:16] = jnp.where(mark & ~is_re, qfix[1], ops[0, 0, 0:16].astype(F32)).astype(BF16)
            ops[0, 0, middle : middle + 16] = jnp.where(
                mark & is_re, swap(qfix[0]), ops[0, 0, middle : middle + 16].astype(F32)
            ).astype(BF16)
        for k in order + [0]:
            at = pl.ds(pl.multiple_of(lax.rem(me + k, n) * band, band), band)
            if split:
                z = mm(cos[at, middle:], ops[0, 0, middle:]) + mm(sin[at, middle:], ops[0, 1, middle:]) + zsum[at]
            else:
                z = mm(cos[at], ops[0, 0]) + mm(sin[at], ops[0, 1])
            if k:
                zsend[j, at] = z.astype(BF16)
                back_copy(j, k).start()
            else:
                zrecv[j, me] = z.astype(BF16)
        if j == 0:
            loads[5].wait()
        else:
            gather(j - 1)
    gather(chunks - 1)

    for j in range(chunks):
        for k in range(1, n):
            forward_copy(j, k).wait_send()
            back_copy(j, k).wait_send()
        if j > 0:
            for half in range(2):
                partner_copy(j, half).wait_send()
    for k in range(n):
        far_copy(k).wait_send()


def local(tiles, pairs, counts):
    n = lax.axis_size("rows")
    nb = lax.axis_size("blk")
    groups, band, width = tiles.shape
    slots = pairs.shape[1]
    height = band * n
    cw = LANES // (2 * groups)
    chunks = width // 2 // n // cw
    cos_h, sin_h = dft_tables(height)
    forward, inverse = row_tables(width, n, cw)
    window = (hann(height)[:, None] * hann(width)[None, :]).reshape(n, band, width)
    vmem = pl.BlockSpec(memory_space=pltpu.VMEM)
    smem = pl.BlockSpec(memory_space=pltpu.SMEM)
    hbm = pl.BlockSpec(memory_space=pltpu.HBM)
    dma = pltpu.SemaphoreType.DMA
    return pl.pallas_call(
        functools.partial(kernel, n, nb, cw),
        out_shape=jax.ShapeDtypeStruct((slots, band, width), F32),
        in_specs=[smem, smem, hbm, hbm, hbm, hbm, hbm, hbm],
        out_specs=vmem,
        scratch_shapes=[
            pltpu.VMEM(tiles.shape, F32),
            pltpu.VMEM((band, width), F32),
            pltpu.VMEM(forward.shape, BF16),
            pltpu.VMEM((height, height), BF16),
            pltpu.VMEM((height, height), BF16),
            pltpu.VMEM(inverse.shape, BF16),
            pltpu.VMEM(tiles.shape, BF16),
            pltpu.VMEM((chunks, n, band, LANES), BF16),
            pltpu.VMEM((chunks, height, LANES), BF16),
            pltpu.VMEM((height, LANES), BF16),
            pltpu.VMEM((2, 2, height, LANES), BF16),
            pltpu.VMEM((chunks, height, LANES), BF16),
            pltpu.VMEM((chunks, height, LANES), BF16),
            pltpu.VMEM((2, 16, LANES), F32),
            pltpu.VMEM((height, LANES), F32),
            pltpu.VMEM((chunks, height, LANES), BF16),
            pltpu.VMEM((chunks, n, band, LANES), BF16),
            dma((6,)),
            dma((chunks, n - 1)),
            dma((chunks, n - 1)),
            dma((n,)),
            dma((n,)),
            dma((chunks, 2)),
            dma((chunks, 2)),
            dma((chunks, n - 1)),
            dma((chunks, n - 1)),
        ],
        compiler_params=pltpu.CompilerParams(
            collective_id=0, has_side_effects=True, vmem_limit_bytes=51 * 1024 * 1024
        ),
    )(
        pairs,
        counts,
        tiles,
        jnp.asarray(window),
        jnp.asarray(forward),
        jnp.asarray(cos_h.astype(ml_dtypes.bfloat16)),
        jnp.asarray(sin_h.astype(ml_dtypes.bfloat16)),
        jnp.asarray(inverse),
    )


def solution(mesh):
    return jax.shard_map(
        local,
        mesh=mesh,
        in_specs=(
            P(("parts", "blk"), "rows", None),
            P(("parts", "blk"), None, None),
            P(("parts", "blk")),
        ),
        out_specs=P(("parts", "blk"), "rows", None),
        check_vma=False,
    )
```
